256 devices in a mesh: ctx: 32 (over z, y), tp: 8 (over x, core).
Axes of the slice: x: 4, y: 4, z: 8, core: 2. Of those that a mesh axis runs over, the one named last changes fastest.
Arguments:
- q_nope: bfloat16 [1, 4096, 8192], P(None, 'ctx', 'tp'), may hold values from -6 to 6
- q_rope: bfloat16 [1, 4096, 4096], P(None, 'ctx', 'tp'), may hold values from -8 to 8
- latent_keys: bfloat16 [1, 4096, 576], P(None, 'ctx'), may hold values from -8 to 8
- group_order: int32 [64], replicated, may hold values from 0 to 63, as said below
- w_uk: bfloat16 [64, 128, 512], P('tp'), may hold values from -0.5 to 0.5
- w_uv: bfloat16 [64, 512, 128], P('tp'), may hold values from -0.25 to 0.25
- o_proj: bfloat16 [8192, 3584], P('tp'), may hold values from -0.0625 to 0.0625
Outputs:
- mixed: bfloat16 [1, 4096, 3584], P(None, 'ctx')
The draws below stay inside these ranges and needn't reach their ends.
Inputs may be any that keep to these rules, and one draw needn't show every extreme that they name: `group_order`: a permutation of the group numbers in which slots 2j and 2j + 1 hold two groups whose numbers add up to 63.
All inputs are finite; a program needn't handle non-finite values.
Results may differ from the reference program's by a relative error of at most 0.02.
Values may be sent and summed in bfloat16 or wider, within the bound.
A program may use at most 128 MiB of HBM per device.

```python
import jax
import jax.numpy as jnp
from jax import lax

SEQS = 1
TOK_CTX = 128
HEADS = 64
NOPE = 128
ROPE = 64
LATENT = 512
VDIM = 128
OUT = 3584
SEQ_LEN = 4096


def slot_groups(key):
    key = jax.random.fold_in(key, 71)
    devices_count = SEQ_LEN // TOK_CTX
    order_key, flip_key = jax.random.split(key)
    paired = jax.random.permutation(order_key, devices_count).astype(jnp.int32)
    flipped = jax.random.randint(flip_key, (devices_count,), 0, 2, dtype=jnp.int32)
    mirror = (2 * devices_count - 1 - paired).astype(jnp.int32)
    first_slot = jnp.where(flipped == 1, mirror, paired)
    second_slot = jnp.where(flipped == 1, paired, mirror)
    return jnp.stack([first_slot, second_slot], 1).reshape(-1).astype(jnp.int32)


def draw_group_order(key, part):
    return slot_groups(key)


def draw_q_rope(key, part):
    key = jax.random.fold_in(key, 9)
    base_key = jax.random.fold_in(key, 0)
    values = jnp.clip(jax.random.normal(base_key, (SEQS, SEQ_LEN, HEADS, ROPE), jnp.float32), -6.0, 6.0)
    return values.reshape(SEQS, SEQ_LEN, HEADS * ROPE).astype(jnp.bfloat16)


def draw_latent_keys(key, part):
    key = jax.random.fold_in(key, 5)
    base_key = jax.random.fold_in(key, 0)
    rope_key = jax.random.fold_in(key, 3)
    latent = jnp.clip(jax.random.normal(base_key, (SEQS, SEQ_LEN, LATENT), jnp.float32), -6.0, 6.0)
    rope_part = jnp.clip(jax.random.normal(rope_key, (SEQS, SEQ_LEN, ROPE), jnp.float32), -6.0, 6.0)
    return jnp.concatenate([latent, rope_part], -1).astype(jnp.bfloat16)


def level_of(key, shape, cuts, smallest, top_value):
    def one(axis_at, parts):
        heights = jax.random.uniform(jax.random.fold_in(jax.random.fold_in(key, 6), axis_at), (parts,), jnp.float32, smallest / len(cuts), top_value / len(cuts))
        return jnp.repeat(jnp.exp(heights), shape[axis_at] // parts).reshape((-1,) + (1,) * (len(shape) - axis_at - 1))

    loudness = one(*cuts[0])
    for cut in cuts[1:]:
        loudness = loudness * one(*cut)
    return loudness


def scatter_about(key, dims, spread, bound, shards=(), kind=jnp.bfloat16):
    array = spread * jax.random.normal(key, dims, jnp.float32)
    if shards:
        array = array * level_of(key, dims, shards, -0.22, 0.18)
    return jnp.clip(array, -bound, bound).astype(kind)


def setup_inputs(seed: int = 0) -> dict:
    streams_of = jax.random.split(jax.random.key(seed), 8)
    q_nope = scatter_about(streams_of[0], (SEQS, SEQ_LEN, HEADS * NOPE), 1.0, 6.0, ((1, 32), (2, 8)))
    q_rope = draw_q_rope(jax.random.fold_in(streams_of[7], 71), 0)
    latent_keys = draw_latent_keys(jax.random.fold_in(streams_of[7], 71), 0)
    group_order = draw_group_order(jax.random.fold_in(streams_of[7], 71), 0)
    w_uk = scatter_about(streams_of[4], (HEADS, NOPE, LATENT), NOPE ** -0.5, 0.5, ((0, 8),))
    w_uv = scatter_about(streams_of[5], (HEADS, LATENT, VDIM), LATENT ** -0.5, 0.25, ((0, 8),))
    o_proj = scatter_about(streams_of[6], (HEADS * VDIM, OUT), (HEADS * VDIM) ** -0.5, 0.0625, ((0, 8),))
    return dict(q_nope=q_nope, q_rope=q_rope, latent_keys=latent_keys, group_order=group_order, w_uk=w_uk, w_uv=w_uv, o_proj=o_proj)


masked_score = -1e30


def token_positions(group_order, length):
    slots = group_order.shape[0]
    width = length // slots
    within = jnp.tile(jnp.arange(width, dtype=jnp.int32), slots)
    return (jnp.repeat(group_order, width) * width + within).astype(jnp.int32)


def rotate(values, positions):
    half_width = values.shape[-1] // 2
    freqs = 10000.0 ** (-jnp.arange(half_width, dtype=jnp.float32) / half_width)
    angles = positions.astype(jnp.float32)[..., None] * freqs
    cosine = jnp.cos(angles)
    sine = jnp.sin(angles)
    first = values[..., :half_width].astype(jnp.float32)
    second = values[..., half_width:].astype(jnp.float32)
    return jnp.concatenate([first * cosine - second * sine, second * cosine + first * sine], -1).astype(jnp.bfloat16)


def reference(q_nope, q_rope, latent_keys, group_order, w_uk, w_uv, o_proj):
    heads, nope_width, latent_width = w_uk.shape
    seqs, length, _ = q_nope.shape
    rope_width = latent_keys.shape[-1] - latent_width
    positions = token_positions(group_order, length)
    queries_nope = q_nope.reshape(seqs, length, heads, nope_width)
    queries_rope = rotate(q_rope.reshape(seqs, length, heads, rope_width), positions[:, None])
    latent = latent_keys[..., :latent_width]
    key_rows = jnp.concatenate([latent, rotate(latent_keys[..., latent_width:], positions)], -1)
    key_rows = lax.optimization_barrier(key_rows)
    absorbed = jnp.einsum("slhn,hnc->slhc", queries_nope.astype(jnp.float32), w_uk.astype(jnp.float32)).astype(jnp.bfloat16)
    queries = lax.optimization_barrier(jnp.concatenate([absorbed, queries_rope], -1))
    score_scale = (nope_width + rope_width) ** -0.5
    visible = positions[None, :] <= positions[:, None]

    def one_head(query_rows):
        scores = jnp.einsum("sqc,skc->sqk", query_rows.astype(jnp.float32), key_rows.astype(jnp.float32)) * score_scale
        scores = jnp.where(visible, scores, masked_score)
        top = jnp.max(scores, -1, keepdims=True)
        weights = jnp.where(visible, jnp.exp(scores - top), 0.0)
        total = jnp.sum(weights, -1, keepdims=True)
        rounded = lax.optimization_barrier(weights.astype(jnp.bfloat16))
        context = jnp.einsum("sqk,skc->sqc", rounded.astype(jnp.float32), latent.astype(jnp.float32)) / total
        return context.astype(jnp.bfloat16)

    contexts = lax.optimization_barrier(lax.map(one_head, jnp.moveaxis(queries, 2, 0)))
    head_out = jnp.einsum("hslc,hcv->slhv", contexts.astype(jnp.float32), w_uv.astype(jnp.float32)).astype(jnp.bfloat16)
    flat = head_out.reshape(seqs * length, heads * w_uv.shape[2])
    mixed = jnp.dot(flat, o_proj, preferred_element_type=jnp.float32).astype(jnp.bfloat16)
    return mixed.reshape(seqs, length, -1)
```

```python
import functools
import math

import jax
import jax.numpy as jnp
import numpy as np
from jax import lax
from jax.experimental import pallas as pl
from jax.experimental.pallas import tpu as pltpu
from jax.sharding import PartitionSpec as P

MESH = pl.DeviceIdType.MESH
NY, NZ, NX = 4, 8, 4
HEADS, NOPE, ROPE, LATENT, VDIM, OUT = 8, 128, 64, 512, 128, 3584
GROUP = 64
TOK = 2 * GROUP
HALF = LATENT // 2
COLS = OUT // 2
SHARDS = NY * NZ
BATCH = 4
BATCHES = SHARDS // BATCH
ROWS = TOK * HEADS
MSG = TOK + 16
KW = LATENT + 128
TILE = 256
HIDDEN = -1e30
SCORE_SCALE = (NOPE + ROPE) ** -0.5 * math.log2(math.e)

TREE = (
    ((0, -1), (0, 0)),
    ((0, 2), (0, 0)),
    ((2, 0), (0, 0)),
    ((3, 0), (0, 0)),
    ((1, 0), (0, 0)),
    ((0, -3), (0, 0)),
    ((0, 1), (0, 0)),
    ((1, -1), (0, -1)),
    ((3, -1), (0, -1)),
    ((0, 3), (0, 2)),
    ((0, -2), (0, -1)),
    ((2, 1), (2, 0)),
    ((2, -1), (2, 0)),
    ((2, -3), (0, -3)),
    ((3, 1), (3, 0)),
    ((1, 1), (0, 1)),
    ((3, -3), (0, -3)),
    ((1, -2), (1, -1)),
    ((0, 4), (0, 3)),
    ((3, 3), (0, 3)),
    ((1, -3), (0, -3)),
    ((2, 2), (2, 1)),
    ((3, -2), (0, -2)),
    ((1, 3), (0, 3)),
    ((2, 4), (2, -3)),
    ((1, 2), (1, 1)),
    ((2, -2), (1, -2)),
    ((3, 2), (3, 3)),
    ((2, 3), (3, 3)),
    ((3, 4), (3, 3)),
    ((1, 4), (0, 4)),
)
SLOT = {(0, 0): 0}
SLOT.update({offset: 1 + at for at, (offset, _) in enumerate(TREE)})
SLOT_OFFSET = [(0, 0)] + [offset for offset, _ in TREE]
KIDS = {}
for _offset, _parent in TREE:
    KIDS.setdefault(_parent, []).append(_offset)


def step_of(offset, parent):
    return ((offset[0] - parent[0]) % NY, (offset[1] - parent[1]) % NZ)


STEPS = sorted({step_of(o, p) for o, p in TREE} | {step_of(p, o) for o, p in TREE})


def dot_nt(a, b):
    return lax.dot_general(a, b, (((1,), (1,)), ((), ())), preferred_element_type=jnp.float32)


def attention_kernel(
    order,
    qn_hbm,
    qr_hbm,
    lk_hbm,
    wuk_hbm,
    wuv_hbm,
    op_hbm,
    out_hbm,
    qn,
    qr,
    lk,
    wuk,
    wuv,
    op,
    kr,
    kbuf,
    qa,
    qb,
    klo,
    khi,
    bias,
    top,
    total,
    acc,
    flat,
    xsend,
    xrecv,
    own,
    part,
    rsr,
    obuf,
    load_sem,
    ring_send,
    ring_recv,
    pair_send,
    pair_recv,
    ex_send,
    ex_recv,
    rs_send,
    rs_recv,
    ag_send,
    ag_recv,
    fw_send,
    fw_recv,
):
    ctx = lax.axis_index("ctx")
    tp = lax.axis_index("tp")
    z, y = ctx // NY, lax.rem(ctx, NY)
    x, c = tp // 2, lax.rem(tp, 2)

    def ring_peer(step):
        dy, dz = step
        return (lax.rem(z + dz, NZ) * NY + lax.rem(y + dy, NY), tp)

    def x_peer(d):
        return (ctx, lax.rem(x + d, NX) * 2 + c)

    partner = (ctx, x * 2 + 1 - c)
    peers = [ring_peer(s) for s in STEPS] + [x_peer(d) for d in (1, 2, 3)] + [partner]
    barrier = pltpu.get_barrier_semaphore()
    for peer in peers:
        pl.semaphore_signal(barrier, inc=1, device_id=peer, device_id_type=MESH)

    loads = [
        pltpu.make_async_copy(src, dst, load_sem.at[at])
        for at, (src, dst) in enumerate(
            [(lk_hbm, lk), (qn_hbm, qn), (qr_hbm, qr), (wuk_hbm, wuk), (wuv_hbm, wuv), (op_hbm, op)]
        )
    ]
    for load in loads:
        load.start()

    g0 = order[2 * ctx]
    g1 = order[2 * ctx + 1]
    swap = g0 > g1
    low = jnp.minimum(g0, g1)

    def sort_rows(value):
        first, second = value[:GROUP], value[GROUP:]
        return jnp.where(swap, second, first), jnp.where(swap, first, second)

    lane = lax.broadcasted_iota(jnp.int32, (TOK, 128), 1)
    row = lax.broadcasted_iota(jnp.int32, (TOK, 128), 0)
    position = jnp.where(row < GROUP, low * GROUP + row, (63 - low) * GROUP + row - GROUP)
    frequencies = np.float32(10000.0) ** (-np.arange(32, dtype=np.float32) / np.float32(32))
    freq_lane = lax.rem(lax.broadcasted_iota(jnp.int32, (8, 128), 1), 32)
    freq = jnp.zeros((8, 128), jnp.float32)
    for at in range(32):
        freq = jnp.where(freq_lane == at, float(frequencies[at]), freq)
    angle = position.astype(jnp.float32) * freq[:1]
    cosine, sine = jnp.cos(angle), jnp.sin(angle)
    first_half = lax.rem(lane, ROPE) < ROPE // 2

    def rotate(value):
        other = jnp.where(first_half, -pltpu.roll(value, 96, 1), pltpu.roll(value, 32, 1))
        return value * cosine + other * sine

    loads[0].wait()
    lat_lo, lat_hi = sort_rows(lk[:, :LATENT])
    for half in range(2):
        kbuf[half, 0, 0:GROUP, :] = lat_lo[:, half * HALF : (half + 1) * HALF]
        kbuf[half, 0, GROUP + 16 : MSG, :] = lat_hi[:, half * HALF : (half + 1) * HALF]
    kr[...] = jnp.zeros_like(kr)
    kr[:, :ROPE] = lk[:, LATENT:].astype(jnp.float32)
    rope_rows = kr[...]
    rope_rows = rope_rows + pltpu.roll(rope_rows, ROPE, 1)
    rotated = rotate(jnp.concatenate(sort_rows(rope_rows), 0))
    packed = jnp.where(lane[:GROUP] < ROPE, rotated[:GROUP], rotated[GROUP:]).astype(jnp.bfloat16)
    for at in range(4):
        kbuf[at // 2, 0, GROUP : GROUP + 16, (at % 2) * 128 : (at % 2 + 1) * 128] = packed[
            at * 16 : (at + 1) * 16
        ]

    pl.semaphore_wait(barrier, len(peers))

    def ring_copy(offset, parent):
        slot = SLOT[offset]
        return pltpu.make_async_remote_copy(
            src_ref=kbuf.at[c, SLOT[parent]],
            dst_ref=kbuf.at[c, slot],
            send_sem=ring_send.at[slot - 1],
            recv_sem=ring_recv.at[slot - 1],
            device_id=ring_peer(step_of(offset, parent)),
            device_id_type=MESH,
        )

    ring = {offset: ring_copy(offset, parent) for offset, parent in TREE}
    for offset in KIDS[(0, 0)]:
        ring[offset].start()

    def pair_copy(batch):
        first = max(1, batch * BATCH)
        rows = kbuf.at[c, pl.ds(first, (batch + 1) * BATCH - first)]
        return pltpu.make_async_remote_copy(
            src_ref=rows,
            dst_ref=rows,
            send_sem=pair_send.at[batch],
            recv_sem=pair_recv.at[batch],
            device_id=partner,
            device_id_type=MESH,
        )

    pairs = [pair_copy(batch) for batch in range(BATCHES)]

    key_lane = lax.broadcasted_iota(jnp.int32, (1, BATCH * GROUP), 1)
    for batch in range(BATCHES):
        low_bias = jnp.zeros((1, BATCH * GROUP), jnp.float32)
        high_bias = jnp.zeros((1, BATCH * GROUP), jnp.float32)
        for at in range(BATCH):
            dy, dz = SLOT_OFFSET[batch * BATCH + at]
            if (dy, dz) == (0, 0):
                continue
            owner = lax.rem(z - dz + NZ, NZ) * NY + lax.rem(y - dy + NY, NY)
            key_low = jnp.minimum(order[2 * owner], order[2 * owner + 1])
            here = key_lane // GROUP == at
            low_bias = jnp.where(here, jnp.where(key_low < low, 0.0, HIDDEN), low_bias)
            high_bias = jnp.where(here, jnp.where(key_low > low, 0.0, HIDDEN), high_bias)
        bias[batch, 0:1, :] = low_bias
        bias[batch, 8:9, :] = high_bias

    top[...] = jnp.full_like(top, HIDDEN)
    total[...] = jnp.zeros_like(total)

    @pl.loop(0, ROWS // GROUP)
    def _(at):
        acc[pl.ds(at * GROUP, GROUP), :] = jnp.zeros((GROUP, LATENT), jnp.float32)

    loads[2].wait()
    for block in range(HEADS // 2):
        rows = qr[:, block * 128 : (block + 1) * 128].astype(jnp.float32)
        rotated = rotate(jnp.concatenate(sort_rows(rows), 0)) * SCORE_SCALE
        shifted = pltpu.roll(rotated, ROPE, 1)
        for odd in range(2):
            head = 2 * block + odd
            for_low = jnp.where(lane < ROPE, shifted if odd else rotated, 0.0).astype(jnp.bfloat16)
            for_high = jnp.where(lane < ROPE, 0.0, rotated if odd else shifted).astype(jnp.bfloat16)
            at = head * GROUP
            qa[at : at + GROUP, LATENT:] = for_low[:GROUP]
            qa[ROWS // 2 + at : ROWS // 2 + at + GROUP, LATENT:] = for_low[GROUP:]
            qb[at : at + GROUP, LATENT:] = for_high[GROUP:]
    loads[1].wait()
    loads[3].wait()
    for head in range(HEADS):
        rows = jnp.concatenate(sort_rows(qn[:, head * NOPE : (head + 1) * NOPE]), 0)
        absorbed = jnp.dot(rows, wuk[head], preferred_element_type=jnp.float32) * SCORE_SCALE
        absorbed = absorbed.astype(jnp.bfloat16)
        at = head * GROUP
        qa[at : at + GROUP, :LATENT] = absorbed[:GROUP]
        qa[ROWS // 2 + at : ROWS // 2 + at + GROUP, :LATENT] = absorbed[GROUP:]
        qb[at : at + GROUP, :LATENT] = absorbed[GROUP:]

    def update(rows, scores, values):
        pieces = [s[:, at : at + 128] for s in scores for at in range(0, s.shape[1], 128)]
        peak = functools.reduce(jnp.maximum, pieces)
        before = top[rows, :]
        now = jnp.maximum(before, jnp.max(peak, 1, keepdims=True))
        fade = jnp.exp2(before - now)
        weights = [jnp.exp2(piece - now) for piece in pieces]
        top[rows, :] = now
        total[rows, :] = total[rows, :] * fade + functools.reduce(jnp.add, weights)
        summed = None
        per = len(weights) // len(values)
        for at, value in enumerate(values):
            mine = jnp.concatenate(
                [w.astype(jnp.bfloat16) for w in weights[at * per : (at + 1) * per]], 1
            )
            part_sum = jnp.dot(mine, value[:, :LATENT], preferred_element_type=jnp.float32)
            summed = part_sum if summed is None else summed + part_sum
        for at in range(0, LATENT, 128):
            acc[rows, at : at + 128] = acc[rows, at : at + 128] * fade + summed[:, at : at + 128]

    def gather_keys(batch):
        for at in range(BATCH):
            slot = batch * BATCH + at
            rows = slice(at * GROUP, (at + 1) * GROUP)
            for half in range(2):
                cols = slice(half * HALF, (half + 1) * HALF)
                klo[rows, cols] = kbuf[half, slot, 0:GROUP, :]
                khi[rows, cols] = kbuf[half, slot, GROUP + 16 : MSG, :]
            for piece in range(4):
                block = kbuf[
                    piece // 2, slot, GROUP : GROUP + 16, (piece % 2) * 128 : (piece % 2 + 1) * 128
                ]
                at_row = at * GROUP + piece * 16
                klo[at_row : at_row + 16, LATENT:] = block
                khi[at_row : at_row + 16, LATENT:] = block

    def own_mask(scores):
        key = lax.broadcasted_iota(jnp.int32, scores.shape, 1)
        token = lax.rem(lax.broadcasted_iota(jnp.int32, scores.shape, 0), GROUP)
        return jnp.where((key < GROUP) & (key > token), HIDDEN, scores)

    def attend_low(batch):
        @pl.loop(0, ROWS // 2 // TILE)
        def _(at):
            rows = pl.ds(pl.multiple_of(at * TILE, TILE), TILE)
            scores = dot_nt(qa[rows, :], klo[...]) + bias[batch, 0:1, :]
            if batch == 0:
                scores = own_mask(scores)
            update(rows, [scores], [klo])

    def attend_high(batch):
        @pl.loop(0, ROWS // 2 // TILE)
        def _(at):
            here = pl.ds(pl.multiple_of(at * TILE, TILE), TILE)
            rows = pl.ds(pl.multiple_of(ROWS // 2 + at * TILE, TILE), TILE)
            on_low = dot_nt(qa[rows, :], klo[...])
            on_high = dot_nt(qb[here, :], khi[...]) + bias[batch, 8:9, :]
            if batch == 0:
                on_high = own_mask(on_high)
            update(rows, [on_low, on_high], [klo, khi])

    mine = pl.multiple_of(c * COLS, 128)
    theirs = pl.multiple_of((1 - c) * COLS, 128)

    def exchange_copy(group):
        return pltpu.make_async_remote_copy(
            src_ref=xsend.at[group],
            dst_ref=xrecv.at[group],
            send_sem=ex_send.at[group],
            recv_sem=ex_recv.at[group],
            device_id=partner,
            device_id_type=MESH,
        )

    def scatter_copy(group, d):
        to = lax.rem(x + d, NX)
        return pltpu.make_async_remote_copy(
            src_ref=part.at[group, pl.ds(pl.multiple_of(to * 16, 16), 16)],
            dst_ref=rsr.at[group, d - 1],
            send_sem=rs_send.at[group, d - 1],
            recv_sem=rs_recv.at[group, d - 1],
            device_id=x_peer(d),
            device_id_type=MESH,
        )

    def out_piece(group, chip, first):
        return obuf.at[
            pl.ds(pl.multiple_of(group * GROUP + chip * 16, 16), 16), pl.ds(first, COLS)
        ]

    def share_copy(group, d):
        piece = out_piece(group, x, mine)
        return pltpu.make_async_remote_copy(
            src_ref=piece,
            dst_ref=piece,
            send_sem=ag_send.at[group, d],
            recv_sem=ag_recv.at[group, d],
            device_id=x_peer(d) if d else partner,
            device_id_type=MESH,
        )

    def forward_copy(group, d):
        piece = out_piece(group, lax.rem(x + NX - d, NX), mine)
        return pltpu.make_async_remote_copy(
            src_ref=piece,
            dst_ref=piece,
            send_sem=fw_send.at[group, d - 1],
            recv_sem=fw_recv.at[group, d - 1],
            device_id=partner,
            device_id_type=MESH,
        )

    def project(group):
        @pl.loop(0, HEADS)
        def _(head):
            rows = pl.ds(pl.multiple_of(group * (ROWS // 2) + head * GROUP, GROUP), GROUP)
            norm = 1.0 / jnp.sum(total[rows, :], 1, keepdims=True)
            context = (acc[rows, :] * norm).astype(jnp.bfloat16)
            flat[group, :, pl.ds(pl.multiple_of(head * VDIM, VDIM), VDIM)] = jnp.dot(
                context, wuv[head], preferred_element_type=jnp.float32
            ).astype(jnp.bfloat16)

        heads = flat[group]

        @pl.loop(0, COLS // TILE)
        def _(at):
            from_cols = pl.ds(pl.multiple_of(theirs + at * TILE, 128), TILE)
            xsend[group, :, pl.ds(pl.multiple_of(at * TILE, TILE), TILE)] = jnp.dot(
                heads, op[:, from_cols], preferred_element_type=jnp.float32
            ).astype(jnp.bfloat16)

        exchange_copy(group).start()

        @pl.loop(0, COLS // TILE)
        def _(at):
            from_cols = pl.ds(pl.multiple_of(mine + at * TILE, 128), TILE)
            own[group, :, pl.ds(pl.multiple_of(at * TILE, TILE), TILE)] = jnp.dot(
                heads, op[:, from_cols], preferred_element_type=jnp.float32
            )

    def scatter(group):
        exchange_copy(group).wait_recv()
        own[group] = own[group] + xrecv[group].astype(jnp.float32)
        part[group] = own[group].astype(jnp.bfloat16)
        for d in (2, 1, 3):
            scatter_copy(group, d).start()

    def share(group):
        for d in (1, 2, 3):
            scatter_copy(group, d).wait_recv()
        rows = pl.ds(pl.multiple_of(x * 16, 16), 16)
        summed = own[group, rows, :]
        for d in range(3):
            summed = summed + rsr[group, d].astype(jnp.float32)
        obuf[
            pl.ds(pl.multiple_of(group * GROUP + x * 16, 16), 16), pl.ds(mine, COLS)
        ] = summed.astype(jnp.bfloat16)
        for d in (2, 1, 3, 0):
            share_copy(group, d).start()

    def forward(group):
        for d in (1, 3, 2):
            share_copy(group, d).wait_recv()
            forward_copy(group, d).start()

    def attend(batch):
        pairs[batch].wait_recv()
        gather_keys(batch)
        attend_low(batch)
        if batch == BATCHES - 1:
            loads[4].wait()
            loads[5].wait()
            project(0)
        attend_high(batch)

    for batch in range(BATCHES):
        for slot in range(max(1, batch * BATCH), (batch + 1) * BATCH):
            offset = SLOT_OFFSET[slot]
            ring[offset].wait_recv()
            for kid in KIDS.get(offset, []):
                ring[kid].start()
        pairs[batch].start()
        if batch:
            attend(batch - 1)
    attend(BATCHES - 1)
    scatter(0)
    project(1)
    scatter(1)
    share(0)
    share(1)
    forward(0)
    forward(1)
    for group in range(2):
        share_copy(group, 0).wait_recv()
        for d in (1, 2, 3):
            forward_copy(group, d).wait_recv()
    done = pltpu.make_async_copy(obuf, out_hbm, load_sem.at[6])
    done.start()
    for offset, _ in TREE:
        ring[offset].wait_send()
    for pair in pairs:
        pair.wait_send()
    for group in range(2):
        exchange_copy(group).wait_send()
        for d in (1, 2, 3):
            scatter_copy(group, d).wait_send()
            share_copy(group, d).wait_send()
            forward_copy(group, d).wait_send()
        share_copy(group, 0).wait_send()
    done.wait()


def on_device(q_nope, q_rope, latent_keys, group_order, w_uk, w_uv, o_proj):
    bf16, f32 = jnp.bfloat16, jnp.float32
    anywhere = pl.BlockSpec(memory_space=pl.ANY)
    vmem, dma = pltpu.VMEM, pltpu.SemaphoreType.DMA
    rows = pl.pallas_call(
        attention_kernel,
        out_shape=jax.ShapeDtypeStruct((TOK, OUT), bf16),
        in_specs=[pl.BlockSpec(memory_space=pltpu.SMEM)] + [anywhere] * 6,
        out_specs=anywhere,
        scratch_shapes=[
            vmem((TOK, HEADS * NOPE), bf16),
            vmem((TOK, HEADS * ROPE), bf16),
            vmem((TOK, LATENT + ROPE), bf16),
            vmem((HEADS, NOPE, LATENT), bf16),
            vmem((HEADS, LATENT, VDIM), bf16),
            vmem((HEADS * VDIM, OUT), bf16),
            vmem((TOK, 128), f32),
            vmem((2, SHARDS, MSG, HALF), bf16),
            vmem((ROWS, KW), bf16),
            vmem((ROWS // 2, KW), bf16),
            vmem((BATCH * GROUP, KW), bf16),
            vmem((BATCH * GROUP, KW), bf16),
            vmem((BATCHES, 16, BATCH * GROUP), f32),
            vmem((ROWS, 128), f32),
            vmem((ROWS, 128), f32),
            vmem((ROWS, LATENT), f32),
            vmem((2, GROUP, HEADS * VDIM), bf16),
            vmem((2, GROUP, COLS), bf16),
            vmem((2, GROUP, COLS), bf16),
            vmem((2, GROUP, COLS), f32),
            vmem((2, GROUP, COLS), bf16),
            vmem((2, 3, 16, COLS), bf16),
            vmem((TOK, OUT), bf16),
            dma((7,)),
            dma((SHARDS - 1,)),
            dma((SHARDS - 1,)),
            dma((BATCHES,)),
            dma((BATCHES,)),
            dma((2,)),
            dma((2,)),
            dma((2, 3)),
            dma((2, 3)),
            dma((2, 4)),
            dma((2, 4)),
            dma((2, 3)),
            dma((2, 3)),
        ],
        compiler_params=pltpu.CompilerParams(
            collective_id=0, has_side_effects=True, vmem_limit_bytes=56 * 1024 * 1024
        ),
    )(
        group_order,
        q_nope.reshape(TOK, HEADS * NOPE),
        q_rope.reshape(TOK, HEADS * ROPE),
        latent_keys.reshape(TOK, LATENT + ROPE),
        w_uk,
        w_uv,
        o_proj,
    )
    pair = lax.dynamic_slice_in_dim(group_order, 2 * lax.axis_index("ctx"), 2)
    halves = rows.reshape(2, GROUP, OUT)
    halves = jnp.where(pair[0] > pair[1], halves[::-1], halves)
    return halves.reshape(1, TOK, OUT)


def solution(mesh):
    placed = (
        P(None, "ctx", "tp"),
        P(None, "ctx", "tp"),
        P(None, "ctx", None),
        P(),
        P("tp", None, None),
        P("tp", None, None),
        P("tp", None),
    )
    return jax.shard_map(
        on_device, mesh=mesh, in_specs=placed, out_specs=P(None, "ctx", None), check_vma=False
    )
```

```python
import functools
import math

import jax
import jax.numpy as jnp
import numpy as np
from jax import lax
from jax.experimental import pallas as pl
from jax.experimental.pallas import tpu as pltpu
from jax.sharding import PartitionSpec as P

MESH = pl.DeviceIdType.MESH
NY, NZ, NX = 4, 8, 4
HEADS, NOPE, ROPE, LATENT, VDIM, OUT = 8, 128, 64, 512, 128, 3584
GROUP = 64
TOK = 2 * GROUP
HALF = LATENT // 2
COLS = OUT // 2
SHARDS = NY * NZ
BATCH = 4
BATCHES = SHARDS // BATCH
ROWS = TOK * HEADS
MSG = TOK + 16
KW = LATENT + 128
PTILE = 896
HIDDEN = -1e30
SCORE_SCALE = (NOPE + ROPE) ** -0.5 * math.log2(math.e)

TREE = (
    ((0, -1), (0, 0)),
    ((0, 2), (0, 0)),
    ((2, 0), (0, 0)),
    ((3, 0), (0, 0)),
    ((1, 0), (0, 0)),
    ((0, -3), (0, 0)),
    ((0, 1), (0, 0)),
    ((1, -1), (0, -1)),
    ((3, -1), (0, -1)),
    ((0, 3), (0, 2)),
    ((0, -2), (0, -1)),
    ((2, 1), (2, 0)),
    ((2, -1), (2, 0)),
    ((2, -3), (0, -3)),
    ((3, 1), (3, 0)),
    ((1, 1), (0, 1)),
    ((3, -3), (0, -3)),
    ((1, -2), (1, -1)),
    ((0, 4), (0, 3)),
    ((3, 3), (0, 3)),
    ((1, -3), (0, -3)),
    ((2, 2), (2, 1)),
    ((3, -2), (0, -2)),
    ((1, 3), (0, 3)),
    ((2, 4), (2, -3)),
    ((1, 2), (1, 1)),
    ((2, -2), (1, -2)),
    ((3, 2), (3, 3)),
    ((2, 3), (3, 3)),
    ((3, 4), (3, 3)),
    ((1, 4), (0, 4)),
)
SLOT = {(0, 0): 0}
SLOT.update({offset: 1 + at for at, (offset, _) in enumerate(TREE)})
SLOT_OFFSET = [(0, 0)] + [offset for offset, _ in TREE]
KIDS = {}
for _offset, _parent in TREE:
    KIDS.setdefault(_parent, []).append(_offset)


def step_of(offset, parent):
    return ((offset[0] - parent[0]) % NY, (offset[1] - parent[1]) % NZ)


STEPS = sorted({step_of(o, p) for o, p in TREE} | {step_of(p, o) for o, p in TREE})


def dot_nt(a, b):
    return lax.dot_general(a, b, (((1,), (1,)), ((), ())), preferred_element_type=jnp.float32)


def attention_kernel(
    order,
    qn_hbm,
    qr_hbm,
    lk_hbm,
    wuk_hbm,
    wuv_hbm,
    op_hbm,
    out,
    qn,
    qr,
    lk,
    wuk,
    wuv,
    op,
    kr,
    kbuf,
    qa,
    qb,
    klo,
    khi,
    bias,
    top,
    total,
    acc,
    flat,
    xsend,
    xrecv,
    own,
    part,
    rsr,
    obuf,
    load_sem,
    ring_send,
    ring_recv,
    pair_send,
    pair_recv,
    ex_send,
    ex_recv,
    rs_send,
    rs_recv,
    ag_send,
    ag_recv,
    fw_send,
    fw_recv,
):
    ctx = lax.axis_index("ctx")
    tp = lax.axis_index("tp")
    z, y = ctx // NY, lax.rem(ctx, NY)
    x, c = tp // 2, lax.rem(tp, 2)

    def ring_peer(step):
        dy, dz = step
        return (lax.rem(z + dz, NZ) * NY + lax.rem(y + dy, NY), tp)

    def x_peer(d):
        return (ctx, lax.rem(x + d, NX) * 2 + c)

    partner = (ctx, x * 2 + 1 - c)
    peers = [ring_peer(s) for s in STEPS] + [x_peer(d) for d in (1, 2, 3)] + [partner]
    barrier = pltpu.get_barrier_semaphore()
    for peer in peers:
        pl.semaphore_signal(barrier, inc=1, device_id=peer, device_id_type=MESH)

    loads = [
        pltpu.make_async_copy(src, dst, load_sem.at[at])
        for at, (src, dst) in enumerate(
            [(lk_hbm, lk), (qn_hbm, qn), (qr_hbm, qr), (wuk_hbm, wuk), (wuv_hbm, wuv), (op_hbm, op)]
        )
    ]
    for load in loads:
        load.start()

    g0 = order[2 * ctx]
    g1 = order[2 * ctx + 1]
    swap = g0 > g1
    low = jnp.minimum(g0, g1)

    def sort_rows(value):
        first, second = value[:GROUP], value[GROUP:]
        return jnp.where(swap, second, first), jnp.where(swap, first, second)

    lane = lax.broadcasted_iota(jnp.int32, (TOK, 128), 1)
    row = lax.broadcasted_iota(jnp.int32, (TOK, 128), 0)
    position = jnp.where(row < GROUP, low * GROUP + row, (63 - low) * GROUP + row - GROUP)
    frequencies = np.float32(10000.0) ** (-np.arange(32, dtype=np.float32) / np.float32(32))
    freq_lane = lax.rem(lax.broadcasted_iota(jnp.int32, (8, 128), 1), 32)
    freq = jnp.zeros((8, 128), jnp.float32)
    for at in range(32):
        freq = jnp.where(freq_lane == at, float(frequencies[at]), freq)
    angle = position.astype(jnp.float32) * freq[:1]
    cosine, sine = jnp.cos(angle), jnp.sin(angle)
    first_half = lax.rem(lane, ROPE) < ROPE // 2

    def rotate(value):
        other = jnp.where(first_half, -pltpu.roll(value, 96, 1), pltpu.roll(value, 32, 1))
        return value * cosine + other * sine

    loads[0].wait()
    keys = jnp.transpose(lk[...].astype(jnp.float32))
    lat_lo, lat_hi = sort_rows(keys[:, :LATENT].astype(jnp.bfloat16))
    for half in range(2):
        kbuf[half, 0, 0:GROUP, :] = lat_lo[:, half * HALF : (half + 1) * HALF]
        kbuf[half, 0, GROUP + 16 : MSG, :] = lat_hi[:, half * HALF : (half + 1) * HALF]
    kr[...] = jnp.zeros_like(kr)
    kr[:, :ROPE] = keys[:, LATENT:]
    rope_rows = kr[...]
    rope_rows = rope_rows + pltpu.roll(rope_rows, ROPE, 1)
    rotated = rotate(jnp.concatenate(sort_rows(rope_rows), 0))
    packed = jnp.where(lane[:GROUP] < ROPE, rotated[:GROUP], rotated[GROUP:]).astype(jnp.bfloat16)
    for at in range(4):
        kbuf[at // 2, 0, GROUP : GROUP + 16, (at % 2) * 128 : (at % 2 + 1) * 128] = packed[
            at * 16 : (at + 1) * 16
        ]

    pl.semaphore_wait(barrier, len(peers))

    def ring_copy(offset, parent):
        slot = SLOT[offset]
        return pltpu.make_async_remote_copy(
            src_ref=kbuf.at[c, SLOT[parent]],
            dst_ref=kbuf.at[c, slot],
            send_sem=ring_send.at[slot - 1],
            recv_sem=ring_recv.at[slot - 1],
            device_id=ring_peer(step_of(offset, parent)),
            device_id_type=MESH,
        )

    ring = {offset: ring_copy(offset, parent) for offset, parent in TREE}
    for offset in KIDS[(0, 0)]:
        ring[offset].start()

    def pair_copy(batch):
        first = max(1, batch * BATCH)
        rows = kbuf.at[c, pl.ds(first, (batch + 1) * BATCH - first)]
        return pltpu.make_async_remote_copy(
            src_ref=rows,
            dst_ref=rows,
            send_sem=pair_send.at[batch],
            recv_sem=pair_recv.at[batch],
            device_id=partner,
            device_id_type=MESH,
        )

    pairs = [pair_copy(batch) for batch in range(BATCHES)]

    key_lane = lax.broadcasted_iota(jnp.int32, (1, BATCH * GROUP), 1)
    for batch in range(BATCHES):
        low_bias = jnp.zeros((1, BATCH * GROUP), jnp.float32)
        high_bias = jnp.zeros((1, BATCH * GROUP), jnp.float32)
        for at in range(BATCH):
            dy, dz = SLOT_OFFSET[batch * BATCH + at]
            if (dy, dz) == (0, 0):
                continue
            owner = lax.rem(z - dz + NZ, NZ) * NY + lax.rem(y - dy + NY, NY)
            key_low = jnp.minimum(order[2 * owner], order[2 * owner + 1])
            here = key_lane // GROUP == at
            low_bias = jnp.where(here, jnp.where(key_low < low, 0.0, HIDDEN), low_bias)
            high_bias = jnp.where(here, jnp.where(key_low > low, 0.0, HIDDEN), high_bias)
        bias[batch, 0:1, :] = low_bias
        bias[batch, 8:9, :] = high_bias

    top[...] = jnp.full_like(top, HIDDEN)
    total[...] = jnp.zeros_like(total)

    @pl.loop(0, ROWS // GROUP)
    def _(at):
        acc[pl.ds(at * GROUP, GROUP), :] = jnp.zeros((GROUP, LATENT), jnp.float32)

    loads[2].wait()
    for block in range(HEADS // 2):
        rows = qr[:, block * 128 : (block + 1) * 128].astype(jnp.float32)
        rotated = rotate(jnp.concatenate(sort_rows(rows), 0)) * SCORE_SCALE
        shifted = pltpu.roll(rotated, ROPE, 1)
        for odd in range(2):
            head = 2 * block + odd
            for_low = jnp.where(lane < ROPE, shifted if odd else rotated, 0.0).astype(jnp.bfloat16)
            for_high = jnp.where(lane < ROPE, 0.0, rotated if odd else shifted).astype(jnp.bfloat16)
            at = head * GROUP
            qa[at : at + GROUP, LATENT:] = for_low[:GROUP]
            qa[ROWS // 2 + at : ROWS // 2 + at + GROUP, LATENT:] = for_low[GROUP:]
            qb[at : at + GROUP, LATENT:] = for_high[GROUP:]
    loads[1].wait()
    loads[3].wait()
    for head in range(HEADS):
        rows = jnp.concatenate(sort_rows(qn[:, head * NOPE : (head + 1) * NOPE]), 0)
        absorbed = jnp.dot(rows, wuk[head], preferred_element_type=jnp.float32) * SCORE_SCALE
        absorbed = absorbed.astype(jnp.bfloat16)
        at = head * GROUP
        qa[at : at + GROUP, :LATENT] = absorbed[:GROUP]
        qa[ROWS // 2 + at : ROWS // 2 + at + GROUP, :LATENT] = absorbed[GROUP:]
        qb[at : at + GROUP, :LATENT] = absorbed[GROUP:]

    def update(rows, scores, values):
        pieces = [s[:, at : at + 128] for s in scores for at in range(0, s.shape[1], 128)]
        peak = functools.reduce(jnp.maximum, pieces)
        before = top[rows, :]
        now = jnp.maximum(before, jnp.max(peak, 1, keepdims=True))
        fade = jnp.exp2(before - now)
        weights = [jnp.exp2(piece - now) for piece in pieces]
        top[rows, :] = now
        total[rows, :] = total[rows, :] * fade + functools.reduce(jnp.add, weights)
        summed = None
        per = len(weights) // len(values)
        for at, value in enumerate(values):
            mine = jnp.concatenate(
                [w.astype(jnp.bfloat16) for w in weights[at * per : (at + 1) * per]], 1
            )
            part_sum = jnp.dot(mine, value[:, :LATENT], preferred_element_type=jnp.float32)
            summed = part_sum if summed is None else summed + part_sum
        for at in range(0, LATENT, 128):
            acc[rows, at : at + 128] = acc[rows, at : at + 128] * fade + summed[:, at : at + 128]

    def gather_keys(batch):
        for at in range(BATCH):
            slot = batch * BATCH + at
            rows = slice(at * GROUP, (at + 1) * GROUP)
            for half in range(2):
                cols = slice(half * HALF, (half + 1) * HALF)
                klo[rows, cols] = kbuf[half, slot, 0:GROUP, :]
                khi[rows, cols] = kbuf[half, slot, GROUP + 16 : MSG, :]
            for piece in range(4):
                block = kbuf[
                    piece // 2, slot, GROUP : GROUP + 16, (piece % 2) * 128 : (piece % 2 + 1) * 128
                ]
                at_row = at * GROUP + piece * 16
                klo[at_row : at_row + 16, LATENT:] = block
                khi[at_row : at_row + 16, LATENT:] = block

    def own_mask(scores):
        key = lax.broadcasted_iota(jnp.int32, scores.shape, 1)
        token = lax.rem(lax.broadcasted_iota(jnp.int32, scores.shape, 0), GROUP)
        return jnp.where((key < GROUP) & (key > token), HIDDEN, scores)

    low_rows, high_rows = pl.ds(0, ROWS // 2), pl.ds(ROWS // 2, ROWS // 2)

    def score_low(batch):
        scores = dot_nt(qa[low_rows, :], klo[...]) + bias[batch, 0:1, :]
        return [own_mask(scores) if batch == 0 else scores]

    def score_high(batch):
        on_low = dot_nt(qa[high_rows, :], klo[...])
        on_high = dot_nt(qb[...], khi[...]) + bias[batch, 8:9, :]
        return [on_low, own_mask(on_high) if batch == 0 else on_high]

    mine = pl.multiple_of(c * COLS, 128)
    theirs = pl.multiple_of((1 - c) * COLS, 128)

    def exchange_copy(group):
        return pltpu.make_async_remote_copy(
            src_ref=xsend.at[group],
            dst_ref=xrecv.at[group],
            send_sem=ex_send.at[group],
            recv_sem=ex_recv.at[group],
            device_id=partner,
            device_id_type=MESH,
        )

    def scatter_copy(group, d):
        to = lax.rem(x + d, NX)
        return pltpu.make_async_remote_copy(
            src_ref=part.at[group, pl.ds(pl.multiple_of(to * 16, 16), 16)],
            dst_ref=rsr.at[group, d - 1],
            send_sem=rs_send.at[group, d - 1],
            recv_sem=rs_recv.at[group, d - 1],
            device_id=x_peer(d),
            device_id_type=MESH,
        )

    def out_piece(group, chip, first):
        return obuf.at[
            pl.ds(pl.multiple_of(group * GROUP + chip * 16, 16), 16), pl.ds(first, COLS)
        ]

    def share_copy(group, d):
        piece = out_piece(group, x, mine)
        return pltpu.make_async_remote_copy(
            src_ref=piece,
            dst_ref=piece,
            send_sem=ag_send.at[group, d],
            recv_sem=ag_recv.at[group, d],
            device_id=x_peer(d) if d else partner,
            device_id_type=MESH,
        )

    def forward_copy(group, d):
        piece = out_piece(group, lax.rem(x + NX - d, NX), mine)
        return pltpu.make_async_remote_copy(
            src_ref=piece,
            dst_ref=piece,
            send_sem=fw_send.at[group, d - 1],
            recv_sem=fw_recv.at[group, d - 1],
            device_id=partner,
            device_id_type=MESH,
        )

    def project(group):
        for head in range(HEADS):
            rows = pl.ds(group * (ROWS // 2) + head * GROUP, GROUP)
            norm = 1.0 / jnp.sum(total[rows, :], 1, keepdims=True)
            context = (acc[rows, :] * norm).astype(jnp.bfloat16)
            flat[group, :, head * VDIM : (head + 1) * VDIM] = jnp.dot(
                context, wuv[head], preferred_element_type=jnp.float32
            ).astype(jnp.bfloat16)

        heads = flat[group]
        for at in range(0, COLS, PTILE):
            from_cols = pl.ds(pl.multiple_of(theirs + at, 128), PTILE)
            xsend[group, :, at : at + PTILE] = jnp.dot(
                heads, op[:, from_cols], preferred_element_type=jnp.float32
            ).astype(jnp.bfloat16)
        exchange_copy(group).start()
        for at in range(0, COLS, PTILE):
            from_cols = pl.ds(pl.multiple_of(mine + at, 128), PTILE)
            own[group, :, at : at + PTILE] = jnp.dot(
                heads, op[:, from_cols], preferred_element_type=jnp.float32
            )

    def scatter(group):
        exchange_copy(group).wait_recv()
        own[group] = own[group] + xrecv[group].astype(jnp.float32)
        part[group] = own[group].astype(jnp.bfloat16)
        for d in (2, 1, 3):
            scatter_copy(group, d).start()

    def share(group):
        for d in (1, 2, 3):
            scatter_copy(group, d).wait_recv()
        rows = pl.ds(pl.multiple_of(x * 16, 16), 16)
        summed = own[group, rows, :]
        for d in range(3):
            summed = summed + rsr[group, d].astype(jnp.float32)
        obuf[
            pl.ds(pl.multiple_of(group * GROUP + x * 16, 16), 16), pl.ds(mine, COLS)
        ] = summed.astype(jnp.bfloat16)
        for d in (2, 1, 3, 0):
            share_copy(group, d).start()

    def forward(group):
        for d in (1, 3, 2):
            share_copy(group, d).wait_recv()
            forward_copy(group, d).start()

    def attend(batch):
        pairs[batch].wait_recv()
        gather_keys(batch)
        low_scores = score_low(batch)
        high_scores = score_high(batch)
        update(low_rows, low_scores, [klo])
        if batch == BATCHES - 1:
            loads[4].wait()
            loads[5].wait()
            project(0)
        update(high_rows, high_scores, [klo, khi])

    for batch in range(BATCHES):
        for slot in range(max(1, batch * BATCH), (batch + 1) * BATCH):
            offset = SLOT_OFFSET[slot]
            ring[offset].wait_recv()
            for kid in KIDS.get(offset, []):
                ring[kid].start()
        pairs[batch].start()
        if batch:
            attend(batch - 1)
    attend(BATCHES - 1)
    scatter(0)
    project(1)
    scatter(1)
    share(0)
    share(1)
    forward(0)
    forward(1)
    for group in range(2):
        share_copy(group, 0).wait_recv()
        for d in (1, 2, 3):
            forward_copy(group, d).wait_recv()
    for piece in range(0, OUT, PTILE):
        cols = slice(piece, piece + PTILE)
        first, second = sort_rows(obuf[:, cols])
        out[:GROUP, cols] = first
        out[GROUP:, cols] = second
    for offset, _ in TREE:
        ring[offset].wait_send()
    for pair in pairs:
        pair.wait_send()
    for group in range(2):
        exchange_copy(group).wait_send()
        for d in (1, 2, 3):
            scatter_copy(group, d).wait_send()
            share_copy(group, d).wait_send()
            forward_copy(group, d).wait_send()
        share_copy(group, 0).wait_send()


def on_device(q_nope, q_rope, latent_keys, group_order, w_uk, w_uv, o_proj):
    bf16, f32 = jnp.bfloat16, jnp.float32
    anywhere = pl.BlockSpec(memory_space=pl.ANY)
    vmem, dma = pltpu.VMEM, pltpu.SemaphoreType.DMA
    rows = pl.pallas_call(
        attention_kernel,
        out_shape=pltpu.VMEM((TOK, OUT), bf16),
        in_specs=[pl.BlockSpec(memory_space=pltpu.SMEM)] + [anywhere] * 6,
        out_specs=pl.BlockSpec(memory_space=pltpu.VMEM),
        scratch_shapes=[
            vmem((TOK, HEADS * NOPE), bf16),
            vmem((TOK, HEADS * ROPE), bf16),
            vmem((LATENT + ROPE, TOK), bf16),
            vmem((HEADS, NOPE, LATENT), bf16),
            vmem((HEADS, LATENT, VDIM), bf16),
            vmem((HEADS * VDIM, OUT), bf16),
            vmem((TOK, 128), f32),
            vmem((2, SHARDS, MSG, HALF), bf16),
            vmem((ROWS, KW), bf16),
            vmem((ROWS // 2, KW), bf16),
            vmem((BATCH * GROUP, KW), bf16),
            vmem((BATCH * GROUP, KW), bf16),
            vmem((BATCHES, 16, BATCH * GROUP), f32),
            vmem((ROWS, 128), f32),
            vmem((ROWS, 128), f32),
            vmem((ROWS, LATENT), f32),
            vmem((2, GROUP, HEADS * VDIM), bf16),
            vmem((2, GROUP, COLS), bf16),
            vmem((2, GROUP, COLS), bf16),
            vmem((2, GROUP, COLS), f32),
            vmem((2, GROUP, COLS), bf16),
            vmem((2, 3, 16, COLS), bf16),
            vmem((TOK, OUT), bf16),
            dma((6,)),
            dma((SHARDS - 1,)),
            dma((SHARDS - 1,)),
            dma((BATCHES,)),
            dma((BATCHES,)),
            dma((2,)),
            dma((2,)),
            dma((2, 3)),
            dma((2, 3)),
            dma((2, 4)),
            dma((2, 4)),
            dma((2, 3)),
            dma((2, 3)),
        ],
        compiler_params=pltpu.CompilerParams(
            collective_id=0, has_side_effects=True, vmem_limit_bytes=56 * 1024 * 1024
        ),
    )(
        group_order,
        q_nope.reshape(TOK, HEADS * NOPE),
        q_rope.reshape(TOK, HEADS * ROPE),
        jnp.transpose(latent_keys, (0, 2, 1)).reshape(LATENT + ROPE, TOK),
        w_uk,
        w_uv,
        o_proj,
    )
    return rows.reshape(1, TOK, OUT)


def solution(mesh):
    placed = (
        P(None, "ctx", "tp"),
        P(None, "ctx", "tp"),
        P(None, "ctx", None),
        P(),
        P("tp", None, None),
        P("tp", None, None),
        P("tp", None),
    )
    return jax.shard_map(
        on_device, mesh=mesh, in_specs=placed, out_specs=P(None, "ctx", None), check_vma=False
    )
```

```python
import functools
import math

import jax
import jax.numpy as jnp
import numpy as np
from jax import lax
from jax.experimental import pallas as pl
from jax.experimental.pallas import tpu as pltpu
from jax.sharding import PartitionSpec as P

MESH = pl.DeviceIdType.MESH
NY, NZ, NX = 4, 8, 4
HEADS, NOPE, ROPE, LATENT, VDIM, OUT = 8, 128, 64, 512, 128, 3584
GROUP = 64
TOK = 2 * GROUP
HALF = LATENT // 2
COLS = OUT // 2
SHARDS = NY * NZ
BATCH = 4
BATCHES = SHARDS // BATCH
ROWS = TOK * HEADS
MSG = TOK + 16
KW = LATENT + 128
PIECES = 2
PIECE = COLS // PIECES
LAST = BATCH * (BATCHES - 1)
HIDDEN = -1e30
SCORE_SCALE = (NOPE + ROPE) ** -0.5 * math.log2(math.e)

TREE = {
    (0, 1): (0, 0),
    (2, 0): (0, 0),
    (1, 0): (0, 0),
    (3, 0): (0, 0),
    (0, 2): (0, 0),
    (0, -3): (0, 0),
    (1, 1): (0, 1),
    (3, 1): (0, 1),
    (2, 1): (2, 0),
    (0, -2): (0, 0),
    (2, -1): (2, 0),
    (0, 3): (0, 2),
    (3, 2): (0, 2),
    (0, -1): (0, 0),
    (1, -1): (1, 0),
    (0, 4): (0, -3),
    (1, 2): (1, 1),
    (1, -2): (0, -2),
    (1, -3): (0, -3),
    (3, -3): (0, -3),
    (2, -2): (2, -1),
    (2, 2): (2, 1),
    (3, -1): (2, -1),
    (3, -2): (0, -2),
    (3, 3): (0, 3),
    (1, 4): (0, 4),
    (1, 3): (0, 3),
    (3, 4): (0, 4),
    (2, 3): (2, 1),
    (2, 4): (2, -1),
    (2, -3): (1, -3),
}
SIDES = {
    (0, -3): 3,
    (0, -2): 1,
    (0, -1): 3,
    (0, 4): 3,
    (1, -2): 1,
    (1, -3): 3,
    (3, -3): 3,
    (3, -2): 3,
    (1, 4): 3,
    (3, 4): 1,
    (2, -3): 1,
}
OFFSETS = (
    (0, 0),
    (0, 1),
    (2, 0),
    (1, 0),
    (3, 0),
    (0, 2),
    (0, -3),
    (1, 1),
    (3, 1),
    (2, 1),
    (0, -2),
    (2, -1),
    (0, 3),
    (3, 2),
    (0, -1),
    (1, -1),
    (0, 4),
    (1, 2),
    (1, -2),
    (1, -3),
    (3, -3),
    (2, -2),
    (2, 2),
    (3, -1),
    (3, -2),
    (3, 3),
    (1, 4),
    (1, 3),
    (3, 4),
    (2, 3),
    (2, 4),
    (2, -3),
)
SENDS = (
    ("half", (0, -3)),
    ("full", (2, 0)),
    ("full", (0, 1)),
    ("full", (0, 2)),
    ("half", (0, -2)),
    ("full", (1, 0)),
    ("half", (0, -1)),
    ("full", (3, 0)),
    ("full", (1, 1)),
    ("full", (3, 1)),
    ("half", (1, -3)),
    ("half", (0, 4)),
    ("side", (0, -3)),
    ("half", (3, -3)),
    ("full", (2, -1)),
    ("full", (2, 1)),
    ("full", (1, -1)),
    ("side", (0, -2)),
    ("half", (1, -2)),
    ("half", (3, -2)),
    ("full", (0, 3)),
    ("full", (3, 2)),
    ("side", (0, -1)),
    ("full", (1, 2)),
    ("side", (0, 4)),
    ("half", (1, 4)),
    ("half", (3, 4)),
    ("side", (1, -3)),
    ("half", (2, -3)),
    ("side", (3, -3)),
    ("full", (2, 2)),
    ("full", (2, 3)),
    ("side", (1, -2)),
    ("side", (3, -2)),
    ("full", (2, -2)),
    ("full", (3, -1)),
    ("full", (2, 4)),
    ("full", (1, 3)),
    ("full", (3, 3)),
    ("side", (1, 4)),
    ("side", (3, 4)),
    ("side", (2, -3)),
)
PLAN = (
    ("full", (0, 1)),
    ("half", (0, -3)),
    ("full", (2, 0)),
    ("full", (1, 0)),
    ("full", (3, 0)),
    ("half", (0, -2)),
    ("full", (0, 2)),
    ("attend", 0),
    ("half", (0, -1)),
    ("side", (0, -3)),
    ("full", (1, 1)),
    ("full", (3, 1)),
    ("half", (0, 4)),
    ("half", (1, -3)),
    ("half", (3, -3)),
    ("full", (2, 1)),
    ("side", (0, -2)),
    ("half", (1, -2)),
    ("half", (3, -2)),
    ("full", (2, -1)),
    ("attend", 1),
    ("full", (0, 3)),
    ("full", (3, 2)),
    ("side", (0, -1)),
    ("full", (1, -1)),
    ("attend", 2),
    ("half", (1, 4)),
    ("half", (3, 4)),
    ("side", (0, 4)),
    ("full", (1, 2)),
    ("half", (2, -3)),
    ("side", (1, -2)),
    ("side", (1, -3)),
    ("attend", 3),
    ("side", (3, -3)),
    ("full", (2, -2)),
    ("full", (2, 2)),
    ("full", (3, -1)),
    ("side", (3, -2)),
    ("attend", 4),
    ("full", (3, 3)),
    ("side", (1, 4)),
    ("full", (1, 3)),
    ("side", (3, 4)),
    ("attend", 5),
    ("full", (2, 3)),
    ("full", (2, 4)),
    ("side", (2, -3)),
    ("attend", 6),
    ("attend", 7, (("heads", 0),)),
    ("heads", 1),
    ("exchange", 0),
    ("exchange", 1),
    ("keep", 0),
    ("scatter", 0, 0),
    ("scatter", 1, 0),
    ("keep", 1),
    ("scatter", 0, 1),
    ("scatter", 1, 1),
    ("settle",),
    ("share", 0, 0),
    ("share", 1, 0),
    ("share", 0, 1),
    ("share", 1, 1),
    ("forward", 0, 0),
    ("forward", 1, 0),
    ("forward", 0, 1),
    ("forward", 1, 1),
)
SLOT = {offset: at for at, offset in enumerate(OFFSETS)}


def step_of(offset, parent):
    return ((offset[0] - parent[0]) % NY, (offset[1] - parent[1]) % NZ)


STEPS = sorted({step_of(o, p) for o, p in TREE.items()} | {step_of(p, o) for o, p in TREE.items()})


def dot_nt(a, b):
    return lax.dot_general(a, b, (((1,), (1,)), ((), ())), preferred_element_type=jnp.float32)


def attention_kernel(
    order,
    qn_hbm,
    qr_hbm,
    lk_hbm,
    wuk_hbm,
    wuv_hbm,
    op_hbm,
    out,
    qn,
    qr,
    lk,
    wuk,
    wuv,
    op,
    kr,
    kbuf,
    qa,
    qb,
    klo,
    khi,
    bias,
    top,
    total,
    acc,
    flat,
    xsend,
    xrecv,
    own,
    part,
    rsr,
    obuf,
    load_sem,
    ring_send,
    ring_recv,
    pair_send,
    pair_recv,
    ex_send,
    ex_recv,
    rs_send,
    rs_recv,
    ag_send,
    ag_recv,
    fw_send,
    fw_recv,
):
    ctx = lax.axis_index("ctx")
    tp = lax.axis_index("tp")
    z, y = ctx // NY, lax.rem(ctx, NY)
    x, c = tp // 2, lax.rem(tp, 2)

    def ring_peer(step):
        dy, dz = step
        return (lax.rem(z + dz, NZ) * NY + lax.rem(y + dy, NY), tp)

    def x_peer(d):
        return (ctx, lax.rem(x + d, NX) * 2 + c)

    partner = (ctx, x * 2 + 1 - c)
    peers = [ring_peer(s) for s in STEPS] + [x_peer(d) for d in (1, 2, 3)] + [partner]
    barrier = pltpu.get_barrier_semaphore()
    for peer in peers:
        pl.semaphore_signal(barrier, inc=1, device_id=peer, device_id_type=MESH)

    loads = [
        pltpu.make_async_copy(src, dst, load_sem.at[at])
        for at, (src, dst) in enumerate(
            [(lk_hbm, lk), (qn_hbm, qn), (qr_hbm, qr), (wuk_hbm, wuk), (wuv_hbm, wuv), (op_hbm, op)]
        )
    ]
    for load in loads:
        load.start()

    g0 = order[2 * ctx]
    g1 = order[2 * ctx + 1]
    swap = g0 > g1
    low = jnp.minimum(g0, g1)

    def sort_rows(value):
        first, second = value[:GROUP], value[GROUP:]
        return jnp.where(swap, second, first), jnp.where(swap, first, second)

    lane = lax.broadcasted_iota(jnp.int32, (TOK, 128), 1)
    row = lax.broadcasted_iota(jnp.int32, (TOK, 128), 0)
    position = jnp.where(row < GROUP, low * GROUP + row, (63 - low) * GROUP + row - GROUP)
    frequencies = np.float32(10000.0) ** (-np.arange(32, dtype=np.float32) / np.float32(32))
    freq_lane = lax.rem(lax.broadcasted_iota(jnp.int32, (8, 128), 1), 32)
    freq = jnp.zeros((8, 128), jnp.float32)
    for at in range(32):
        freq = jnp.where(freq_lane == at, float(frequencies[at]), freq)
    angle = position.astype(jnp.float32) * freq[:1]
    cosine, sine = jnp.cos(angle), jnp.sin(angle)
    first_half = lax.rem(lane, ROPE) < ROPE // 2

    def rotate(value):
        other = jnp.where(first_half, -pltpu.roll(value, 96, 1), pltpu.roll(value, 32, 1))
        return value * cosine + other * sine

    loads[0].wait()
    keys = jnp.transpose(lk[...].astype(jnp.float32))
    lat_lo, lat_hi = sort_rows(keys[:, :LATENT].astype(jnp.bfloat16))
    for half in range(2):
        kbuf[half, 0, 0:GROUP, :] = lat_lo[:, half * HALF : (half + 1) * HALF]
        kbuf[half, 0, GROUP + 16 : MSG, :] = lat_hi[:, half * HALF : (half + 1) * HALF]
    kr[...] = jnp.zeros_like(kr)
    kr[:, :ROPE] = keys[:, LATENT:]
    rope_rows = kr[...]
    rope_rows = rope_rows + pltpu.roll(rope_rows, ROPE, 1)
    rotated = rotate(jnp.concatenate(sort_rows(rope_rows), 0))
    packed = jnp.where(lane[:GROUP] < ROPE, rotated[:GROUP], rotated[GROUP:]).astype(jnp.bfloat16)
    for at in range(4):
        kbuf[at // 2, 0, GROUP : GROUP + 16, (at % 2) * 128 : (at % 2 + 1) * 128] = packed[
            at * 16 : (at + 1) * 16
        ]

    pl.semaphore_wait(barrier, len(peers))

    def ring_block(offset, kind, other=False):
        if kind == "full":
            return kbuf.at[c, SLOT[offset]]
        parity = lax.rem(x, 2)
        first = (1 - parity if other else parity) * (HALF // 2)
        return kbuf.at[c, SLOT[offset], :, pl.ds(pl.multiple_of(first, 128), HALF // 2)]

    def ring_copy(kind, offset, arriving=False):
        side = kind == "side"
        sem = (SHARDS if side else 0) + SLOT[offset]
        return pltpu.make_async_remote_copy(
            src_ref=ring_block(offset if side else TREE[offset], kind, arriving and side),
            dst_ref=ring_block(offset, kind, arriving and side),
            send_sem=ring_send.at[sem],
            recv_sem=ring_recv.at[sem],
            device_id=x_peer(SIDES[offset]) if side else ring_peer(step_of(offset, TREE[offset])),
            device_id_type=MESH,
        )

    ring = {send: ring_copy(*send) for send in SENDS}

    def hand_on(kind, offset):
        for send in SENDS:
            if send[0] == "side":
                if kind == "half" and send[1] == offset:
                    ring[send].start()
            elif kind != "side" and TREE[send[1]] == offset:
                ring[send].start()

    hand_on("full", (0, 0))

    def pair_copy(first, count):
        rows = kbuf.at[c, pl.ds(first, count)]
        return pltpu.make_async_remote_copy(
            src_ref=rows,
            dst_ref=rows,
            send_sem=pair_send.at[first],
            recv_sem=pair_recv.at[first],
            device_id=partner,
            device_id_type=MESH,
        )

    spans = [(max(1, at), min(at + BATCH, SHARDS) - max(1, at)) for at in range(0, LAST, BATCH)]
    spans += [(at, 1) for at in range(LAST, SHARDS)]
    pairs = {first + count - 1: pair_copy(first, count) for first, count in spans}

    key_lane = lax.broadcasted_iota(jnp.int32, (1, BATCH * GROUP), 1)

    def mask_row(offsets, visible):
        line = jnp.zeros((1, BATCH * GROUP), jnp.float32)
        for at, (dy, dz) in enumerate(offsets):
            if (dy, dz) != (0, 0):
                owner = lax.rem(z - dz + NZ, NZ) * NY + lax.rem(y - dy + NY, NY)
                key_low = jnp.minimum(order[2 * owner], order[2 * owner + 1])
                here = key_lane // GROUP == at
                line = jnp.where(here, jnp.where(visible(key_low), 0.0, HIDDEN), line)
        return line

    for batch in range(BATCHES):
        span = slice(batch * BATCH, (batch + 1) * BATCH)
        bias[batch, 0:1, :] = mask_row(OFFSETS[span], lambda key_low: key_low < low)
        bias[batch, 8:9, :] = mask_row(OFFSETS[span], lambda key_low: key_low > low)

    top[...] = jnp.full_like(top, HIDDEN)
    total[...] = jnp.zeros_like(total)

    @pl.loop(0, ROWS // GROUP)
    def _(at):
        acc[pl.ds(at * GROUP, GROUP), :] = jnp.zeros((GROUP, LATENT), jnp.float32)

    loads[2].wait()
    for block in range(HEADS // 2):
        rows = qr[:, block * 128 : (block + 1) * 128].astype(jnp.float32)
        rotated = rotate(jnp.concatenate(sort_rows(rows), 0)) * SCORE_SCALE
        shifted = pltpu.roll(rotated, ROPE, 1)
        for odd in range(2):
            head = 2 * block + odd
            for_low = jnp.where(lane < ROPE, shifted if odd else rotated, 0.0).astype(jnp.bfloat16)
            for_high = jnp.where(lane < ROPE, 0.0, rotated if odd else shifted).astype(jnp.bfloat16)
            at = head * GROUP
            qa[at : at + GROUP, LATENT:] = for_low[:GROUP]
            qa[ROWS // 2 + at : ROWS // 2 + at + GROUP, LATENT:] = for_low[GROUP:]
            qb[at : at + GROUP, LATENT:] = for_high[GROUP:]
    loads[1].wait()
    loads[3].wait()
    for head in range(HEADS):
        rows = jnp.concatenate(sort_rows(qn[:, head * NOPE : (head + 1) * NOPE]), 0)
        absorbed = jnp.dot(rows, wuk[head], preferred_element_type=jnp.float32) * SCORE_SCALE
        absorbed = absorbed.astype(jnp.bfloat16)
        at = head * GROUP
        qa[at : at + GROUP, :LATENT] = absorbed[:GROUP]
        qa[ROWS // 2 + at : ROWS // 2 + at + GROUP, :LATENT] = absorbed[GROUP:]
        qb[at : at + GROUP, :LATENT] = absorbed[GROUP:]

    def update(rows, scores, values):
        pieces = [s[:, at : at + 128] for s in scores for at in range(0, s.shape[1], 128)]
        peak = functools.reduce(jnp.maximum, pieces)
        before = top[rows, :]
        now = jnp.maximum(before, jnp.max(peak, 1, keepdims=True))
        fade = jnp.exp2(before - now)
        weights = [jnp.exp2(piece - now) for piece in pieces]
        top[rows, :] = now
        total[rows, :] = total[rows, :] * fade + functools.reduce(jnp.add, weights)
        summed = None
        per = len(weights) // len(values)
        for at, value in enumerate(values):
            mine = jnp.concatenate(
                [w.astype(jnp.bfloat16) for w in weights[at * per : (at + 1) * per]], 1
            )
            part_sum = jnp.dot(mine, value[:, :LATENT], preferred_element_type=jnp.float32)
            summed = part_sum if summed is None else summed + part_sum
        for at in range(0, LATENT, 128):
            acc[rows, at : at + 128] = acc[rows, at : at + 128] * fade + summed[:, at : at + 128]

    def gather_keys(batch):
        for at in range(BATCH):
            slot = batch * BATCH + at
            rows = slice(at * GROUP, (at + 1) * GROUP)
            for half in range(2):
                cols = slice(half * HALF, (half + 1) * HALF)
                klo[rows, cols] = kbuf[half, slot, 0:GROUP, :]
                khi[rows, cols] = kbuf[half, slot, GROUP + 16 : MSG, :]
            for piece in range(4):
                rotary = kbuf[
                    piece // 2, slot, GROUP : GROUP + 16, (piece % 2) * 128 : (piece % 2 + 1) * 128
                ]
                at_row = at * GROUP + piece * 16
                klo[at_row : at_row + 16, LATENT:] = rotary
                khi[at_row : at_row + 16, LATENT:] = rotary

    def own_mask(scores):
        key = lax.broadcasted_iota(jnp.int32, scores.shape, 1)
        token = lax.rem(lax.broadcasted_iota(jnp.int32, scores.shape, 0), GROUP)
        return jnp.where((key < GROUP) & (key > token), HIDDEN, scores)

    low_rows, high_rows = pl.ds(0, ROWS // 2), pl.ds(ROWS // 2, ROWS // 2)

    def score(batch):
        for slot in range(batch * BATCH, (batch + 1) * BATCH):
            if slot in pairs:
                pairs[slot].wait_recv()
        gather_keys(batch)
        low_low = dot_nt(qa[low_rows, :], klo[...]) + bias[batch, 0:1, :]
        high_low = dot_nt(qa[high_rows, :], klo[...])
        high_high = dot_nt(qb[...], khi[...]) + bias[batch, 8:9, :]
        if batch == 0:
            low_low, high_high = own_mask(low_low), own_mask(high_high)
        return [low_low], [high_low, high_high]

    def attend(batch, between=()):
        low_scores, high_scores = score(batch)
        update(low_rows, low_scores, [klo])
        for step in between:
            run(step)
        update(high_rows, high_scores, [klo, khi])

    def column(core, piece):
        return pl.multiple_of(core * COLS + piece * PIECE, 128)

    def exchange_copy(group, piece):
        return pltpu.make_async_remote_copy(
            src_ref=xsend.at[group, piece],
            dst_ref=xrecv.at[group, piece],
            send_sem=ex_send.at[group, piece],
            recv_sem=ex_recv.at[group, piece],
            device_id=partner,
            device_id_type=MESH,
        )

    def scatter_copy(group, piece, d):
        to = lax.rem(x + d, NX)
        return pltpu.make_async_remote_copy(
            src_ref=part.at[group, piece, pl.ds(pl.multiple_of(to * 16, 16), 16)],
            dst_ref=rsr.at[group, piece, d - 1],
            send_sem=rs_send.at[group, piece, d - 1],
            recv_sem=rs_recv.at[group, piece, d - 1],
            device_id=x_peer(d),
            device_id_type=MESH,
        )

    def out_piece(group, piece, chip):
        rows = pl.ds(pl.multiple_of(group * GROUP + chip * 16, 16), 16)
        return obuf.at[rows, pl.ds(column(c, piece), PIECE)]

    def share_copy(group, piece, d):
        block = out_piece(group, piece, x)
        return pltpu.make_async_remote_copy(
            src_ref=block,
            dst_ref=block,
            send_sem=ag_send.at[group, piece, d],
            recv_sem=ag_recv.at[group, piece, d],
            device_id=x_peer(d) if d else partner,
            device_id_type=MESH,
        )

    def forward_copy(group, piece, d):
        block = out_piece(group, piece, lax.rem(x + NX - d, NX))
        return pltpu.make_async_remote_copy(
            src_ref=block,
            dst_ref=block,
            send_sem=fw_send.at[group, piece, d - 1],
            recv_sem=fw_recv.at[group, piece, d - 1],
            device_id=partner,
            device_id_type=MESH,
        )

    def heads(group):
        if group == 0:
            loads[4].wait()
            loads[5].wait()
        for head in range(HEADS):
            rows = pl.ds(group * (ROWS // 2) + head * GROUP, GROUP)
            norm = 1.0 / jnp.sum(total[rows, :], 1, keepdims=True)
            context = (acc[rows, :] * norm).astype(jnp.bfloat16)
            flat[group * GROUP : (group + 1) * GROUP, head * VDIM : (head + 1) * VDIM] = jnp.dot(
                context, wuv[head], preferred_element_type=jnp.float32
            ).astype(jnp.bfloat16)

    def partial_out(core, piece):
        return jnp.dot(
            flat[...], op[:, pl.ds(column(core, piece), PIECE)], preferred_element_type=jnp.float32
        )

    def exchange(piece):
        sums = partial_out(1 - c, piece).astype(jnp.bfloat16)
        for group in range(2):
            xsend[group, piece] = sums[group * GROUP : (group + 1) * GROUP]
            exchange_copy(group, piece).start()

    def keep(piece):
        sums = partial_out(c, piece)
        for group in range(2):
            own[group, piece] = sums[group * GROUP : (group + 1) * GROUP]

    def scatter(group, piece):
        exchange_copy(group, piece).wait_recv()
        summed = own[group, piece] + xrecv[group, piece].astype(jnp.float32)
        own[group, piece] = summed
        part[group, piece] = summed.astype(jnp.bfloat16)
        for d in (2, 1, 3):
            scatter_copy(group, piece, d).start()

    def share(group, piece):
        for d in (1, 2, 3):
            scatter_copy(group, piece, d).wait_recv()
        summed = own[group, piece, pl.ds(pl.multiple_of(x * 16, 16), 16), :]
        for d in range(3):
            summed = summed + rsr[group, piece, d].astype(jnp.float32)
        rows = pl.ds(pl.multiple_of(group * GROUP + x * 16, 16), 16)
        obuf[rows, pl.ds(column(c, piece), PIECE)] = summed.astype(jnp.bfloat16)
        for d in (2, 1, 3, 0):
            share_copy(group, piece, d).start()

    def forward(group, piece):
        for d in (1, 3, 2):
            share_copy(group, piece, d).wait_recv()
            forward_copy(group, piece, d).start()

    def settle_gather():
        for send in SENDS:
            ring[send].wait_send()
        for pair in pairs.values():
            pair.wait_send()

    def arrive(kind, offset):
        (ring_copy(kind, offset, True) if kind == "side" else ring[kind, offset]).wait_recv()
        hand_on(kind, offset)
        if kind != "half" and SLOT[offset] in pairs:
            pairs[SLOT[offset]].start()

    steps = {
        "attend": attend,
        "heads": heads,
        "exchange": exchange,
        "keep": keep,
        "scatter": scatter,
        "share": share,
        "forward": forward,
        "settle": settle_gather,
    }

    def run(step):
        if step[0] in steps:
            steps[step[0]](*step[1:])
        else:
            arrive(*step)

    for step in PLAN:
        run(step)

    tail = [(group, piece) for group in range(2) for piece in range(PIECES)]
    for group, piece in tail:
        share_copy(group, piece, 0).wait_recv()
        for d in (1, 2, 3):
            forward_copy(group, piece, d).wait_recv()
    for at in range(0, OUT, PIECE):
        cols = slice(at, at + PIECE)
        first, second = sort_rows(obuf[:, cols])
        out[:GROUP, cols] = first
        out[GROUP:, cols] = second
    for group, piece in tail:
        exchange_copy(group, piece).wait_send()
        share_copy(group, piece, 0).wait_send()
        for d in (1, 2, 3):
            scatter_copy(group, piece, d).wait_send()
            share_copy(group, piece, d).wait_send()
            forward_copy(group, piece, d).wait_send()


def on_device(q_nope, q_rope, latent_keys, group_order, w_uk, w_uv, o_proj):
    bf16, f32 = jnp.bfloat16, jnp.float32
    anywhere = pl.BlockSpec(memory_space=pl.ANY)
    vmem, dma = pltpu.VMEM, pltpu.SemaphoreType.DMA
    rows = pl.pallas_call(
        attention_kernel,
        out_shape=pltpu.VMEM((TOK, OUT), bf16),
        in_specs=[pl.BlockSpec(memory_space=pltpu.SMEM)] + [anywhere] * 6,
        out_specs=pl.BlockSpec(memory_space=pltpu.VMEM),
        scratch_shapes=[
            vmem((TOK, HEADS * NOPE), bf16),
            vmem((TOK, HEADS * ROPE), bf16),
            vmem((LATENT + ROPE, TOK), bf16),
            vmem((HEADS, NOPE, LATENT), bf16),
            vmem((HEADS, LATENT, VDIM), bf16),
            vmem((HEADS * VDIM, OUT), bf16),
            vmem((TOK, 128), f32),
            vmem((2, SHARDS, MSG, HALF), bf16),
            vmem((ROWS, KW), bf16),
            vmem((ROWS // 2, KW), bf16),
            vmem((BATCH * GROUP, KW), bf16),
            vmem((BATCH * GROUP, KW), bf16),
            vmem((BATCHES, 16, BATCH * GROUP), f32),
            vmem((ROWS, 128), f32),
            vmem((ROWS, 128), f32),
            vmem((ROWS, LATENT), f32),
            vmem((TOK, HEADS * VDIM), bf16),
            vmem((2, PIECES, GROUP, PIECE), bf16),
            vmem((2, PIECES, GROUP, PIECE), bf16),
            vmem((2, PIECES, GROUP, PIECE), f32),
            vmem((2, PIECES, GROUP, PIECE), bf16),
            vmem((2, PIECES, 3, 16, PIECE), bf16),
            vmem((TOK, OUT), bf16),
            dma((6,)),
            dma((2 * SHARDS,)),
            dma((2 * SHARDS,)),
            dma((SHARDS,)),
            dma((SHARDS,)),
            dma((2, PIECES)),
            dma((2, PIECES)),
            dma((2, PIECES, 3)),
            dma((2, PIECES, 3)),
            dma((2, PIECES, 4)),
            dma((2, PIECES, 4)),
            dma((2, PIECES, 3)),
            dma((2, PIECES, 3)),
        ],
        compiler_params=pltpu.CompilerParams(
            collective_id=0, has_side_effects=True, vmem_limit_bytes=56 * 1024 * 1024
        ),
    )(
        group_order,
        q_nope.reshape(TOK, HEADS * NOPE),
        q_rope.reshape(TOK, HEADS * ROPE),
        jnp.transpose(latent_keys, (0, 2, 1)).reshape(LATENT + ROPE, TOK),
        w_uk,
        w_uv,
        o_proj,
    )
    return rows.reshape(1, TOK, OUT)


def solution(mesh):
    placed = (
        P(None, "ctx", "tp"),
        P(None, "ctx", "tp"),
        P(None, "ctx", None),
        P(),
        P("tp", None, None),
        P("tp", None, None),
        P("tp", None),
    )
    return jax.shard_map(
        on_device, mesh=mesh, in_specs=placed, out_specs=P(None, "ctx", None), check_vma=False
    )
```

```python
import functools
import math

import jax
import jax.numpy as jnp
import numpy as np
from jax import lax
from jax.experimental import pallas as pl
from jax.experimental.pallas import tpu as pltpu
from jax.sharding import PartitionSpec as P

MESH = pl.DeviceIdType.MESH
NY, NZ, NX = 4, 8, 4
HEADS, NOPE, ROPE, LATENT, VDIM, OUT = 8, 128, 64, 512, 128, 3584
GROUP = 64
TOK = 2 * GROUP
HALF = LATENT // 2
COLS = OUT // 2
SHARDS = NY * NZ
BATCH = 4
BATCHES = SHARDS // BATCH
ROWS = TOK * HEADS
MSG = TOK + 16
KW = LATENT + 128
PIECES = 2
PIECE = COLS // PIECES
LAST = BATCH * (BATCHES - 1)
HIDDEN = -1e30
SCORE_SCALE = (NOPE + ROPE) ** -0.5 * math.log2(math.e)

TREE = {
    (0, 1): (0, 0),
    (2, 0): (0, 0),
    (1, 0): (0, 0),
    (3, 0): (0, 0),
    (0, 2): (0, 0),
    (0, -3): (0, 0),
    (1, 1): (0, 1),
    (3, 1): (0, 1),
    (2, 1): (2, 0),
    (0, -2): (0, 0),
    (2, -1): (2, 0),
    (0, 3): (0, 2),
    (3, 2): (0, 2),
    (0, -1): (0, 0),
    (1, -1): (1, 0),
    (0, 4): (0, -3),
    (1, 2): (1, 1),
    (1, -2): (0, -2),
    (1, -3): (0, -3),
    (3, -3): (0, -3),
    (2, -2): (2, -1),
    (2, 2): (2, 1),
    (3, -1): (2, -1),
    (3, -2): (0, -2),
    (3, 3): (0, 3),
    (1, 4): (0, 4),
    (1, 3): (0, 3),
    (3, 4): (0, 4),
    (2, 3): (2, 1),
    (2, 4): (2, -1),
    (2, -3): (1, -3),
}
SIDES = {
    (0, -3): 3,
    (0, -2): 1,
    (0, -1): 3,
    (0, 4): 3,
    (1, -2): 1,
    (1, -3): 3,
    (3, -3): 3,
    (3, -2): 3,
    (1, 4): 3,
    (3, 4): 1,
    (2, -3): 1,
}
OFFSETS = (
    (0, 0),
    (0, 1),
    (2, 0),
    (1, 0),
    (3, 0),
    (0, 2),
    (0, -3),
    (1, 1),
    (3, 1),
    (2, 1),
    (0, -2),
    (2, -1),
    (0, 3),
    (3, 2),
    (0, -1),
    (1, -1),
    (0, 4),
    (1, 2),
    (1, -2),
    (1, -3),
    (3, -3),
    (2, -2),
    (2, 2),
    (3, -1),
    (3, -2),
    (3, 3),
    (1, 4),
    (1, 3),
    (3, 4),
    (2, 3),
    (2, 4),
    (2, -3),
)
SENDS = (
    ("half", (0, -3)),
    ("full", (2, 0)),
    ("full", (0, 1)),
    ("full", (0, 2)),
    ("half", (0, -2)),
    ("full", (1, 0)),
    ("half", (0, -1)),
    ("full", (3, 0)),
    ("full", (1, 1)),
    ("full", (3, 1)),
    ("half", (1, -3)),
    ("half", (0, 4)),
    ("side", (0, -3)),
    ("half", (3, -3)),
    ("full", (2, -1)),
    ("full", (2, 1)),
    ("full", (1, -1)),
    ("side", (0, -2)),
    ("half", (1, -2)),
    ("half", (3, -2)),
    ("full", (0, 3)),
    ("full", (3, 2)),
    ("side", (0, -1)),
    ("full", (1, 2)),
    ("side", (0, 4)),
    ("half", (1, 4)),
    ("half", (3, 4)),
    ("side", (1, -3)),
    ("half", (2, -3)),
    ("side", (3, -3)),
    ("full", (2, 2)),
    ("full", (2, 3)),
    ("side", (1, -2)),
    ("side", (3, -2)),
    ("full", (2, -2)),
    ("full", (3, -1)),
    ("full", (2, 4)),
    ("full", (1, 3)),
    ("full", (3, 3)),
    ("side", (1, 4)),
    ("side", (3, 4)),
    ("side", (2, -3)),
)
PLAN = (
    ("full", (0, 1)),
    ("half", (0, -3)),
    ("full", (2, 0)),
    ("full", (1, 0)),
    ("full", (3, 0)),
    ("half", (0, -2)),
    ("full", (0, 2)),
    ("attend", 0),
    ("half", (0, -1)),
    ("side", (0, -3)),
    ("full", (1, 1)),
    ("full", (3, 1)),
    ("half", (0, 4)),
    ("half", (1, -3)),
    ("half", (3, -3)),
    ("full", (2, 1)),
    ("side", (0, -2)),
    ("half", (1, -2)),
    ("half", (3, -2)),
    ("full", (2, -1)),
    ("attend", 1),
    ("full", (0, 3)),
    ("full", (3, 2)),
    ("side", (0, -1)),
    ("full", (1, -1)),
    ("attend", 2),
    ("half", (1, 4)),
    ("half", (3, 4)),
    ("side", (0, 4)),
    ("full", (1, 2)),
    ("half", (2, -3)),
    ("side", (1, -2)),
    ("side", (1, -3)),
    ("attend", 3),
    ("side", (3, -3)),
    ("full", (2, -2)),
    ("full", (2, 2)),
    ("full", (3, -1)),
    ("side", (3, -2)),
    ("attend", 4),
    ("full", (3, 3)),
    ("side", (1, 4)),
    ("full", (1, 3)),
    ("side", (3, 4)),
    ("attend", 5),
    ("full", (2, 3)),
    ("full", (2, 4)),
    ("side", (2, -3)),
    ("attend", 6),
    ("attend", 7, (("heads", 0),)),
    ("heads", 1),
    ("slots",),
    ("exchange", 0),
    ("exchange", 1),
    ("keep", 0),
    ("scatter", 0, 0),
    ("scatter", 1, 0),
    ("keep", 1),
    ("scatter", 0, 1),
    ("scatter", 1, 1),
    ("settle_gather",),
    ("share", 0, 0),
    ("share", 1, 0),
    ("share", 0, 1),
    ("share", 1, 1),
    ("settle_output",),
    ("forward", 0, 0),
    ("forward", 1, 0),
    ("forward", 0, 1),
    ("forward", 1, 1),
)
SLOT = {offset: at for at, offset in enumerate(OFFSETS)}


def step_of(offset, parent):
    return ((offset[0] - parent[0]) % NY, (offset[1] - parent[1]) % NZ)


STEPS = sorted({step_of(o, p) for o, p in TREE.items()} | {step_of(p, o) for o, p in TREE.items()})


def dot_nt(a, b):
    return lax.dot_general(a, b, (((1,), (1,)), ((), ())), preferred_element_type=jnp.float32)


def attention_kernel(
    order,
    qn_hbm,
    qr_hbm,
    lk_hbm,
    wuk_hbm,
    wuv_hbm,
    op_hbm,
    out,
    qn,
    qr,
    lk,
    wuk,
    wuv,
    op,
    kr,
    kbuf,
    qa,
    qb,
    klo,
    khi,
    bias,
    top,
    total,
    acc,
    flat,
    xsend,
    xrecv,
    own,
    part,
    rsr,
    load_sem,
    ring_send,
    ring_recv,
    pair_send,
    pair_recv,
    ex_send,
    ex_recv,
    rs_send,
    rs_recv,
    ag_send,
    ag_recv,
    fw_send,
    fw_recv,
):
    ctx = lax.axis_index("ctx")
    tp = lax.axis_index("tp")
    z, y = ctx // NY, lax.rem(ctx, NY)
    x, c = tp // 2, lax.rem(tp, 2)

    def ring_peer(step):
        dy, dz = step
        return (lax.rem(z + dz, NZ) * NY + lax.rem(y + dy, NY), tp)

    def x_peer(d):
        return (ctx, lax.rem(x + d, NX) * 2 + c)

    partner = (ctx, x * 2 + 1 - c)
    peers = [ring_peer(s) for s in STEPS] + [x_peer(d) for d in (1, 2, 3)] + [partner]
    barrier = pltpu.get_barrier_semaphore()
    for peer in peers:
        pl.semaphore_signal(barrier, inc=1, device_id=peer, device_id_type=MESH)

    loads = [
        pltpu.make_async_copy(src, dst, load_sem.at[at])
        for at, (src, dst) in enumerate(
            [(lk_hbm, lk), (qn_hbm, qn), (qr_hbm, qr), (wuk_hbm, wuk), (wuv_hbm, wuv), (op_hbm, op)]
        )
    ]
    for load in loads:
        load.start()

    g0 = order[2 * ctx]
    g1 = order[2 * ctx + 1]
    swap = g0 > g1
    low = jnp.minimum(g0, g1)

    def sort_rows(value):
        first, second = value[:GROUP], value[GROUP:]
        return jnp.where(swap, second, first), jnp.where(swap, first, second)

    lane = lax.broadcasted_iota(jnp.int32, (TOK, 128), 1)
    row = lax.broadcasted_iota(jnp.int32, (TOK, 128), 0)
    position = jnp.where(row < GROUP, low * GROUP + row, (63 - low) * GROUP + row - GROUP)
    frequencies = np.float32(10000.0) ** (-np.arange(32, dtype=np.float32) / np.float32(32))
    freq_lane = lax.rem(lax.broadcasted_iota(jnp.int32, (8, 128), 1), 32)
    freq = jnp.zeros((8, 128), jnp.float32)
    for at in range(32):
        freq = jnp.where(freq_lane == at, float(frequencies[at]), freq)
    angle = position.astype(jnp.float32) * freq[:1]
    cosine, sine = jnp.cos(angle), jnp.sin(angle)
    first_half = lax.rem(lane, ROPE) < ROPE // 2

    def rotate(value):
        other = jnp.where(first_half, -pltpu.roll(value, 96, 1), pltpu.roll(value, 32, 1))
        return value * cosine + other * sine

    loads[0].wait()
    keys = jnp.transpose(lk[...].astype(jnp.float32))
    lat_lo, lat_hi = sort_rows(keys[:, :LATENT].astype(jnp.bfloat16))
    for half in range(2):
        kbuf[half, 0, 0:GROUP, :] = lat_lo[:, half * HALF : (half + 1) * HALF]
        kbuf[half, 0, GROUP + 16 : MSG, :] = lat_hi[:, half * HALF : (half + 1) * HALF]
    kr[...] = jnp.zeros_like(kr)
    kr[:, :ROPE] = keys[:, LATENT:]
    rope_rows = kr[...]
    rope_rows = rope_rows + pltpu.roll(rope_rows, ROPE, 1)
    rotated = rotate(jnp.concatenate(sort_rows(rope_rows), 0))
    packed = jnp.where(lane[:GROUP] < ROPE, rotated[:GROUP], rotated[GROUP:]).astype(jnp.bfloat16)
    for at in range(4):
        kbuf[at // 2, 0, GROUP : GROUP + 16, (at % 2) * 128 : (at % 2 + 1) * 128] = packed[
            at * 16 : (at + 1) * 16
        ]

    pl.semaphore_wait(barrier, len(peers))

    def ring_block(offset, kind, other=False):
        if kind == "full":
            return kbuf.at[c, SLOT[offset]]
        parity = lax.rem(x, 2)
        first = (1 - parity if other else parity) * (HALF // 2)
        return kbuf.at[c, SLOT[offset], :, pl.ds(pl.multiple_of(first, 128), HALF // 2)]

    def ring_copy(kind, offset, arriving=False):
        side = kind == "side"
        sem = (SHARDS if side else 0) + SLOT[offset]
        return pltpu.make_async_remote_copy(
            src_ref=ring_block(offset if side else TREE[offset], kind, arriving and side),
            dst_ref=ring_block(offset, kind, arriving and side),
            send_sem=ring_send.at[sem],
            recv_sem=ring_recv.at[sem],
            device_id=x_peer(SIDES[offset]) if side else ring_peer(step_of(offset, TREE[offset])),
            device_id_type=MESH,
        )

    ring = {send: ring_copy(*send) for send in SENDS}

    def hand_on(kind, offset):
        for send in SENDS:
            if send[0] == "side":
                if kind == "half" and send[1] == offset:
                    ring[send].start()
            elif kind != "side" and TREE[send[1]] == offset:
                ring[send].start()

    hand_on("full", (0, 0))

    def pair_copy(first, count):
        rows = kbuf.at[c, pl.ds(first, count)]
        return pltpu.make_async_remote_copy(
            src_ref=rows,
            dst_ref=rows,
            send_sem=pair_send.at[first],
            recv_sem=pair_recv.at[first],
            device_id=partner,
            device_id_type=MESH,
        )

    spans = [(max(1, at), min(at + BATCH, SHARDS) - max(1, at)) for at in range(0, LAST, BATCH)]
    spans += [(at, 1) for at in range(LAST, SHARDS)]
    pairs = {first + count - 1: pair_copy(first, count) for first, count in spans}

    key_lane = lax.broadcasted_iota(jnp.int32, (1, BATCH * GROUP), 1)

    def mask_row(offsets, visible):
        line = jnp.zeros((1, BATCH * GROUP), jnp.float32)
        for at, (dy, dz) in enumerate(offsets):
            if (dy, dz) != (0, 0):
                owner = lax.rem(z - dz + NZ, NZ) * NY + lax.rem(y - dy + NY, NY)
                key_low = jnp.minimum(order[2 * owner], order[2 * owner + 1])
                here = key_lane // GROUP == at
                line = jnp.where(here, jnp.where(visible(key_low), 0.0, HIDDEN), line)
        return line

    for batch in range(BATCHES):
        span = slice(batch * BATCH, (batch + 1) * BATCH)
        bias[batch, 0:1, :] = mask_row(OFFSETS[span], lambda key_low: key_low < low)
        bias[batch, 8:9, :] = mask_row(OFFSETS[span], lambda key_low: key_low > low)

    top[...] = jnp.full_like(top, HIDDEN)
    total[...] = jnp.zeros_like(total)

    @pl.loop(0, ROWS // GROUP)
    def _(at):
        acc[pl.ds(at * GROUP, GROUP), :] = jnp.zeros((GROUP, LATENT), jnp.float32)

    loads[2].wait()
    for block in range(HEADS // 2):
        rows = qr[:, block * 128 : (block + 1) * 128].astype(jnp.float32)
        rotated = rotate(jnp.concatenate(sort_rows(rows), 0)) * SCORE_SCALE
        shifted = pltpu.roll(rotated, ROPE, 1)
        for odd in range(2):
            head = 2 * block + odd
            for_low = jnp.where(lane < ROPE, shifted if odd else rotated, 0.0).astype(jnp.bfloat16)
            for_high = jnp.where(lane < ROPE, 0.0, rotated if odd else shifted).astype(jnp.bfloat16)
            at = head * GROUP
            qa[at : at + GROUP, LATENT:] = for_low[:GROUP]
            qa[ROWS // 2 + at : ROWS // 2 + at + GROUP, LATENT:] = for_low[GROUP:]
            qb[at : at + GROUP, LATENT:] = for_high[GROUP:]
    loads[1].wait()
    loads[3].wait()
    for head in range(HEADS):
        rows = jnp.concatenate(sort_rows(qn[:, head * NOPE : (head + 1) * NOPE]), 0)
        absorbed = jnp.dot(rows, wuk[head], preferred_element_type=jnp.float32) * SCORE_SCALE
        absorbed = absorbed.astype(jnp.bfloat16)
        at = head * GROUP
        qa[at : at + GROUP, :LATENT] = absorbed[:GROUP]
        qa[ROWS // 2 + at : ROWS // 2 + at + GROUP, :LATENT] = absorbed[GROUP:]
        qb[at : at + GROUP, :LATENT] = absorbed[GROUP:]

    def soften(rows, scores):
        pieces = [s[:, at : at + 128] for s in scores for at in range(0, s.shape[1], 128)]
        peak = functools.reduce(jnp.maximum, pieces)
        before = top[rows, :]
        now = jnp.maximum(before, jnp.max(peak, 1, keepdims=True))
        fade = jnp.exp2(before - now)
        weights = [jnp.exp2(piece - now) for piece in pieces]
        top[rows, :] = now
        total[rows, :] = total[rows, :] * fade + functools.reduce(jnp.add, weights)
        return fade, [w.astype(jnp.bfloat16) for w in weights]

    def gain(rows, softened, values):
        fade, weights = softened
        summed = None
        per = len(weights) // len(values)
        for at, value in enumerate(values):
            mine = jnp.concatenate(weights[at * per : (at + 1) * per], 1)
            part_sum = jnp.dot(mine, value[:, :LATENT], preferred_element_type=jnp.float32)
            summed = part_sum if summed is None else summed + part_sum
        for at in range(0, LATENT, 128):
            acc[rows, at : at + 128] = acc[rows, at : at + 128] * fade + summed[:, at : at + 128]

    def gather_keys(batch):
        for at in range(BATCH):
            slot = batch * BATCH + at
            rows = slice(at * GROUP, (at + 1) * GROUP)
            for half in range(2):
                cols = slice(half * HALF, (half + 1) * HALF)
                klo[rows, cols] = kbuf[half, slot, 0:GROUP, :]
                khi[rows, cols] = kbuf[half, slot, GROUP + 16 : MSG, :]
            for piece in range(4):
                rotary = kbuf[
                    piece // 2, slot, GROUP : GROUP + 16, (piece % 2) * 128 : (piece % 2 + 1) * 128
                ]
                at_row = at * GROUP + piece * 16
                klo[at_row : at_row + 16, LATENT:] = rotary
                khi[at_row : at_row + 16, LATENT:] = rotary

    def own_mask(scores):
        key = lax.broadcasted_iota(jnp.int32, scores.shape, 1)
        token = lax.rem(lax.broadcasted_iota(jnp.int32, scores.shape, 0), GROUP)
        return jnp.where((key < GROUP) & (key > token), HIDDEN, scores)

    low_rows, high_rows = pl.ds(0, ROWS // 2), pl.ds(ROWS // 2, ROWS // 2)

    def attend(batch, between=()):
        for slot in range(batch * BATCH, (batch + 1) * BATCH):
            if slot in pairs:
                pairs[slot].wait_recv()
        gather_keys(batch)

        def low_low(rows=low_rows):
            scores = dot_nt(qa[rows, :], klo[...]) + bias[batch, 0:1, :]
            return own_mask(scores) if batch == 0 else scores

        def high_low(rows=high_rows):
            return dot_nt(qa[rows, :], klo[...])

        def high_high(rows=pl.ds(0, ROWS // 2)):
            scores = dot_nt(qb[rows, :], khi[...]) + bias[batch, 8:9, :]
            return own_mask(scores) if batch == 0 else scores

        n = ROWS // 4
        a, b = pl.ds(0, n), pl.ds(n, n)
        ha, hb = pl.ds(2 * n, n), pl.ds(3 * n, n)
        la = low_low(a)
        lb = low_low(b)
        wa = soften(a, [la])
        hla, hha = high_low(ha), high_high(a)
        wb = soften(b, [lb])
        gain(a, wa, [klo])
        hlb, hhb = high_low(hb), high_high(b)
        wha = soften(ha, [hla, hha])
        gain(b, wb, [klo])
        for step in between:
            run(step)
        whb = soften(hb, [hlb, hhb])
        gain(ha, wha, [klo, khi])
        gain(hb, whb, [klo, khi])

    def column(core, piece):
        return pl.multiple_of(core * COLS + piece * PIECE, 128)

    def exchange_copy(group, piece):
        return pltpu.make_async_remote_copy(
            src_ref=xsend.at[group, piece],
            dst_ref=xrecv.at[group, piece],
            send_sem=ex_send.at[group, piece],
            recv_sem=ex_recv.at[group, piece],
            device_id=partner,
            device_id_type=MESH,
        )

    def scatter_copy(group, piece, d):
        to = lax.rem(x + d, NX)
        return pltpu.make_async_remote_copy(
            src_ref=part.at[group, piece, pl.ds(pl.multiple_of(to * 16, 16), 16)],
            dst_ref=rsr.at[group, piece, d - 1],
            send_sem=rs_send.at[group, piece, d - 1],
            recv_sem=rs_recv.at[group, piece, d - 1],
            device_id=x_peer(d),
            device_id_type=MESH,
        )

    def out_piece(group, piece, chip):
        rows = pl.ds(pl.multiple_of(group * GROUP + chip * 16, 16), 16)
        return out.at[rows, pl.ds(column(c, piece), PIECE)]

    def share_copy(group, piece, d):
        block = out_piece(group, piece, x)
        return pltpu.make_async_remote_copy(
            src_ref=block,
            dst_ref=block,
            send_sem=ag_send.at[group, piece, d],
            recv_sem=ag_recv.at[group, piece, d],
            device_id=x_peer(d) if d else partner,
            device_id_type=MESH,
        )

    def forward_copy(group, piece, d):
        block = out_piece(group, piece, lax.rem(x + NX - d, NX))
        return pltpu.make_async_remote_copy(
            src_ref=block,
            dst_ref=block,
            send_sem=fw_send.at[group, piece, d - 1],
            recv_sem=fw_recv.at[group, piece, d - 1],
            device_id=partner,
            device_id_type=MESH,
        )

    def heads(group):
        if group == 0:
            loads[4].wait()
            loads[5].wait()
        for head in range(HEADS):
            rows = pl.ds(group * (ROWS // 2) + head * GROUP, GROUP)
            norm = 1.0 / jnp.sum(total[rows, :], 1, keepdims=True)
            context = (acc[rows, :] * norm).astype(jnp.bfloat16)
            flat[group * GROUP : (group + 1) * GROUP, head * VDIM : (head + 1) * VDIM] = jnp.dot(
                context, wuv[head], preferred_element_type=jnp.float32
            ).astype(jnp.bfloat16)

    def to_slots():
        first, second = sort_rows(flat[...])
        flat[:GROUP], flat[GROUP:] = first, second

    def partial_out(core, piece):
        return jnp.dot(
            flat[...], op[:, pl.ds(column(core, piece), PIECE)], preferred_element_type=jnp.float32
        )

    def exchange(piece):
        sums = partial_out(1 - c, piece).astype(jnp.bfloat16)
        for group in range(2):
            xsend[group, piece] = sums[group * GROUP : (group + 1) * GROUP]
            exchange_copy(group, piece).start()

    def keep(piece):
        sums = partial_out(c, piece)
        for group in range(2):
            own[group, piece] = sums[group * GROUP : (group + 1) * GROUP]

    def scatter(group, piece):
        exchange_copy(group, piece).wait_recv()
        summed = own[group, piece] + xrecv[group, piece].astype(jnp.float32)
        own[group, piece] = summed
        part[group, piece] = summed.astype(jnp.bfloat16)
        for d in (2, 1, 3):
            scatter_copy(group, piece, d).start()

    def share(group, piece):
        for d in (1, 2, 3):
            scatter_copy(group, piece, d).wait_recv()
        summed = own[group, piece, pl.ds(pl.multiple_of(x * 16, 16), 16), :]
        for d in range(3):
            summed = summed + rsr[group, piece, d].astype(jnp.float32)
        rows = pl.ds(pl.multiple_of(group * GROUP + x * 16, 16), 16)
        out[rows, pl.ds(column(c, piece), PIECE)] = summed.astype(jnp.bfloat16)
        for d in (2, 1, 3, 0):
            share_copy(group, piece, d).start()

    def forward(group, piece):
        for d in (1, 3, 2):
            share_copy(group, piece, d).wait_recv()
            forward_copy(group, piece, d).start()

    def settle_output():
        for group in range(2):
            for piece in range(PIECES):
                exchange_copy(group, piece).wait_send()
                for d in (1, 2, 3):
                    scatter_copy(group, piece, d).wait_send()

    def settle_gather():
        for send in SENDS:
            ring[send].wait_send()
        for pair in pairs.values():
            pair.wait_send()

    def arrive(kind, offset):
        (ring_copy(kind, offset, True) if kind == "side" else ring[kind, offset]).wait_recv()
        hand_on(kind, offset)
        if kind != "half" and SLOT[offset] in pairs:
            pairs[SLOT[offset]].start()

    steps = {
        "attend": attend,
        "heads": heads,
        "exchange": exchange,
        "keep": keep,
        "scatter": scatter,
        "share": share,
        "forward": forward,
        "slots": to_slots,
        "settle_gather": settle_gather,
        "settle_output": settle_output,
    }

    def run(step):
        if step[0] in steps:
            steps[step[0]](*step[1:])
        else:
            arrive(*step)

    for step in PLAN:
        run(step)

    tail = [(group, piece) for group in range(2) for piece in range(PIECES)]
    for group, piece in tail:
        share_copy(group, piece, 0).wait_recv()
        for d in (1, 2, 3):
            forward_copy(group, piece, d).wait_recv()
    for group, piece in tail:
        for d in (0, 1, 2, 3):
            share_copy(group, piece, d).wait_send()
        for d in (1, 2, 3):
            forward_copy(group, piece, d).wait_send()


def on_device(q_nope, q_rope, latent_keys, group_order, w_uk, w_uv, o_proj):
    bf16, f32 = jnp.bfloat16, jnp.float32
    anywhere = pl.BlockSpec(memory_space=pl.ANY)
    vmem, dma = pltpu.VMEM, pltpu.SemaphoreType.DMA
    rows = pl.pallas_call(
        attention_kernel,
        out_shape=pltpu.VMEM((TOK, OUT), bf16),
        in_specs=[pl.BlockSpec(memory_space=pltpu.SMEM)] + [anywhere] * 6,
        out_specs=pl.BlockSpec(memory_space=pltpu.VMEM),
        scratch_shapes=[
            vmem((TOK, HEADS * NOPE), bf16),
            vmem((TOK, HEADS * ROPE), bf16),
            vmem((LATENT + ROPE, TOK), bf16),
            vmem((HEADS, NOPE, LATENT), bf16),
            vmem((HEADS, LATENT, VDIM), bf16),
            vmem((HEADS * VDIM, OUT), bf16),
            vmem((TOK, 128), f32),
            vmem((2, SHARDS, MSG, HALF), bf16),
            vmem((ROWS, KW), bf16),
            vmem((ROWS // 2, KW), bf16),
            vmem((BATCH * GROUP, KW), bf16),
            vmem((BATCH * GROUP, KW), bf16),
            vmem((BATCHES, 16, BATCH * GROUP), f32),
            vmem((ROWS, 128), f32),
            vmem((ROWS, 128), f32),
            vmem((ROWS, LATENT), f32),
            vmem((TOK, HEADS * VDIM), bf16),
            vmem((2, PIECES, GROUP, PIECE), bf16),
            vmem((2, PIECES, GROUP, PIECE), bf16),
            vmem((2, PIECES, GROUP, PIECE), f32),
            vmem((2, PIECES, GROUP, PIECE), bf16),
            vmem((2, PIECES, 3, 16, PIECE), bf16),
            dma((6,)),
            dma((2 * SHARDS,)),
            dma((2 * SHARDS,)),
            dma((SHARDS,)),
            dma((SHARDS,)),
            dma((2, PIECES)),
            dma((2, PIECES)),
            dma((2, PIECES, 3)),
            dma((2, PIECES, 3)),
            dma((2, PIECES, 4)),
            dma((2, PIECES, 4)),
            dma((2, PIECES, 3)),
            dma((2, PIECES, 3)),
        ],
        compiler_params=pltpu.CompilerParams(
            collective_id=0, has_side_effects=True, vmem_limit_bytes=56 * 1024 * 1024
        ),
    )(
        group_order,
        q_nope.reshape(TOK, HEADS * NOPE),
        q_rope.reshape(TOK, HEADS * ROPE),
        jnp.transpose(latent_keys, (0, 2, 1)).reshape(LATENT + ROPE, TOK),
        w_uk,
        w_uv,
        o_proj,
    )
    return rows.reshape(1, TOK, OUT)


def solution(mesh):
    placed = (
        P(None, "ctx", "tp"),
        P(None, "ctx", "tp"),
        P(None, "ctx", None),
        P(),
        P("tp", None, None),
        P("tp", None, None),
        P("tp", None),
    )
    return jax.shard_map(
        on_device, mesh=mesh, in_specs=placed, out_specs=P(None, "ctx", None), check_vma=False
    )
```

```python
import functools
import math

import jax
import jax.numpy as jnp
import numpy as np
from jax import lax
from jax.experimental import pallas as pl
from jax.experimental.pallas import tpu as pltpu
from jax.sharding import PartitionSpec as P

MESH = pl.DeviceIdType.MESH
NY, NZ, NX = 4, 8, 4
HEADS, NOPE, ROPE, LATENT, VDIM, OUT = 8, 128, 64, 512, 128, 3584
GROUP = 64
TOK = 2 * GROUP
HALF = LATENT // 2
COLS = OUT // 2
SHARDS = NY * NZ
BATCH = 4
BATCHES = SHARDS // BATCH
ROWS = TOK * HEADS
MSG = TOK + 16
KW = LATENT + 128
PIECES = 1
PIECE = COLS // PIECES
LAST = BATCH * (BATCHES - 1)
HIDDEN = -1e30
SCORE_SCALE = (NOPE + ROPE) ** -0.5 * math.log2(math.e)

TREE = {
    (0, 1): (0, 0),
    (2, 0): (0, 0),
    (1, 0): (0, 0),
    (3, 0): (0, 0),
    (0, 2): (0, 0),
    (0, -3): (0, 0),
    (1, 1): (0, 1),
    (3, 1): (0, 1),
    (2, 1): (2, 0),
    (0, -2): (0, 0),
    (2, -1): (2, 0),
    (0, 3): (0, 2),
    (3, 2): (0, 2),
    (0, -1): (0, 0),
    (1, -1): (1, 0),
    (0, 4): (0, -3),
    (1, 2): (1, 1),
    (1, -2): (0, -2),
    (1, -3): (0, -3),
    (3, -3): (0, -3),
    (2, -2): (2, -1),
    (2, 2): (2, 1),
    (3, -1): (2, -1),
    (3, -2): (0, -2),
    (3, 3): (0, 3),
    (1, 4): (0, 4),
    (1, 3): (0, 3),
    (3, 4): (0, 4),
    (2, 3): (2, 1),
    (2, 4): (2, -1),
    (2, -3): (1, -3),
}
SIDES = {
    (0, -3): 3,
    (0, -2): 1,
    (0, -1): 3,
    (0, 4): 3,
    (1, -2): 1,
    (1, -3): 3,
    (3, -3): 3,
    (3, -2): 3,
    (1, 4): 3,
    (3, 4): 1,
    (2, -3): 1,
}
OFFSETS = (
    (0, 0),
    (0, 1),
    (2, 0),
    (1, 0),
    (3, 0),
    (0, 2),
    (0, -3),
    (1, 1),
    (3, 1),
    (2, 1),
    (0, -2),
    (2, -1),
    (0, 3),
    (3, 2),
    (0, -1),
    (1, -1),
    (0, 4),
    (1, 2),
    (1, -2),
    (1, -3),
    (3, -3),
    (2, -2),
    (2, 2),
    (3, -1),
    (3, -2),
    (3, 3),
    (1, 4),
    (1, 3),
    (3, 4),
    (2, 3),
    (2, 4),
    (2, -3),
)
SENDS = (
    ("half", (0, -3)),
    ("full", (2, 0)),
    ("full", (0, 1)),
    ("full", (0, 2)),
    ("half", (0, -2)),
    ("full", (1, 0)),
    ("half", (0, -1)),
    ("full", (3, 0)),
    ("full", (1, 1)),
    ("full", (3, 1)),
    ("half", (1, -3)),
    ("half", (0, 4)),
    ("side", (0, -3)),
    ("half", (3, -3)),
    ("full", (2, -1)),
    ("full", (2, 1)),
    ("full", (1, -1)),
    ("side", (0, -2)),
    ("half", (1, -2)),
    ("half", (3, -2)),
    ("full", (0, 3)),
    ("full", (3, 2)),
    ("side", (0, -1)),
    ("full", (1, 2)),
    ("side", (0, 4)),
    ("half", (1, 4)),
    ("half", (3, 4)),
    ("side", (1, -3)),
    ("half", (2, -3)),
    ("side", (3, -3)),
    ("full", (2, 2)),
    ("full", (2, 3)),
    ("side", (1, -2)),
    ("side", (3, -2)),
    ("full", (2, -2)),
    ("full", (3, -1)),
    ("full", (2, 4)),
    ("full", (1, 3)),
    ("full", (3, 3)),
    ("side", (1, 4)),
    ("side", (3, 4)),
    ("side", (2, -3)),
)
PLAN = (
    ("full", (0, 1)),
    ("half", (0, -3)),
    ("full", (2, 0)),
    ("full", (1, 0)),
    ("full", (3, 0)),
    ("half", (0, -2)),
    ("full", (0, 2)),
    ("attend", 0),
    ("half", (0, -1)),
    ("side", (0, -3)),
    ("full", (1, 1)),
    ("full", (3, 1)),
    ("half", (0, 4)),
    ("half", (1, -3)),
    ("half", (3, -3)),
    ("full", (2, 1)),
    ("side", (0, -2)),
    ("half", (1, -2)),
    ("half", (3, -2)),
    ("full", (2, -1)),
    ("attend", 1),
    ("full", (0, 3)),
    ("full", (3, 2)),
    ("side", (0, -1)),
    ("full", (1, -1)),
    ("attend", 2),
    ("half", (1, 4)),
    ("half", (3, 4)),
    ("side", (0, 4)),
    ("full", (1, 2)),
    ("half", (2, -3)),
    ("side", (1, -2)),
    ("side", (1, -3)),
    ("attend", 3),
    ("side", (3, -3)),
    ("full", (2, -2)),
    ("full", (2, 2)),
    ("full", (3, -1)),
    ("side", (3, -2)),
    ("attend", 4),
    ("full", (3, 3)),
    ("side", (1, 4)),
    ("full", (1, 3)),
    ("side", (3, 4)),
    ("attend", 5),
    ("full", (2, 3)),
    ("full", (2, 4)),
    ("side", (2, -3)),
    ("attend", 6),
    ("attend", 7, (("heads", 0),)),
    ("heads", 1),
    ("slots",),
    ("exchange", 0),
    ("keep", 0),
    ("scatter", 0, 0),
    ("scatter", 1, 0),
    ("settle_gather",),
    ("share", 0, 0),
    ("share", 1, 0),
    ("settle_output",),
    ("forward", 0, 0),
    ("forward", 1, 0),
)
SLOT = {offset: at for at, offset in enumerate(OFFSETS)}


def step_of(offset, parent):
    return ((offset[0] - parent[0]) % NY, (offset[1] - parent[1]) % NZ)


STEPS = sorted({step_of(o, p) for o, p in TREE.items()} | {step_of(p, o) for o, p in TREE.items()})


def dot_nt(a, b):
    return lax.dot_general(a, b, (((1,), (1,)), ((), ())), preferred_element_type=jnp.float32)


def attention_kernel(
    order,
    qn_hbm,
    qr_hbm,
    lk_hbm,
    wuk_hbm,
    wuv_hbm,
    op_hbm,
    out,
    qn,
    qr,
    lk,
    wuk,
    wuv,
    op,
    kr,
    kbuf,
    qa,
    qb,
    klo,
    khi,
    bias,
    top,
    total,
    acc,
    flat,
    xsend,
    xrecv,
    own,
    part,
    rsr,
    load_sem,
    ring_send,
    ring_recv,
    pair_send,
    pair_recv,
    ex_send,
    ex_recv,
    rs_send,
    rs_recv,
    ag_send,
    ag_recv,
    fw_send,
    fw_recv,
):
    ctx = lax.axis_index("ctx")
    tp = lax.axis_index("tp")
    z, y = ctx // NY, lax.rem(ctx, NY)
    x, c = tp // 2, lax.rem(tp, 2)

    def ring_peer(step):
        dy, dz = step
        return (lax.rem(z + dz, NZ) * NY + lax.rem(y + dy, NY), tp)

    def x_peer(d):
        return (ctx, lax.rem(x + d, NX) * 2 + c)

    partner = (ctx, x * 2 + 1 - c)
    peers = [ring_peer(s) for s in STEPS] + [x_peer(d) for d in (1, 2, 3)] + [partner]
    barrier = pltpu.get_barrier_semaphore()
    for peer in peers:
        pl.semaphore_signal(barrier, inc=1, device_id=peer, device_id_type=MESH)

    loads = [
        pltpu.make_async_copy(src, dst, load_sem.at[at])
        for at, (src, dst) in enumerate(
            [(lk_hbm, lk), (qn_hbm, qn), (qr_hbm, qr), (wuk_hbm, wuk), (wuv_hbm, wuv), (op_hbm, op)]
        )
    ]
    for load in loads:
        load.start()

    g0 = order[2 * ctx]
    g1 = order[2 * ctx + 1]
    swap = g0 > g1
    low = jnp.minimum(g0, g1)

    def sort_rows(value):
        first, second = value[:GROUP], value[GROUP:]
        return jnp.where(swap, second, first), jnp.where(swap, first, second)

    lane = lax.broadcasted_iota(jnp.int32, (TOK, 128), 1)
    row = lax.broadcasted_iota(jnp.int32, (TOK, 128), 0)
    position = jnp.where(row < GROUP, low * GROUP + row, (63 - low) * GROUP + row - GROUP)
    frequencies = np.float32(10000.0) ** (-np.arange(32, dtype=np.float32) / np.float32(32))
    freq_lane = lax.rem(lax.broadcasted_iota(jnp.int32, (8, 128), 1), 32)
    freq = jnp.zeros((8, 128), jnp.float32)
    for at in range(32):
        freq = jnp.where(freq_lane == at, float(frequencies[at]), freq)
    angle = position.astype(jnp.float32) * freq[:1]
    cosine, sine = jnp.cos(angle), jnp.sin(angle)
    first_half = lax.rem(lane, ROPE) < ROPE // 2

    def rotate(value):
        other = jnp.where(first_half, -pltpu.roll(value, 96, 1), pltpu.roll(value, 32, 1))
        return value * cosine + other * sine

    loads[0].wait()
    keys = jnp.transpose(lk[...].astype(jnp.float32))
    lat_lo, lat_hi = sort_rows(keys[:, :LATENT].astype(jnp.bfloat16))
    for half in range(2):
        kbuf[half, 0, 0:GROUP, :] = lat_lo[:, half * HALF : (half + 1) * HALF]
        kbuf[half, 0, GROUP + 16 : MSG, :] = lat_hi[:, half * HALF : (half + 1) * HALF]
    kr[...] = jnp.zeros_like(kr)
    kr[:, :ROPE] = keys[:, LATENT:]
    rope_rows = kr[...]
    rope_rows = rope_rows + pltpu.roll(rope_rows, ROPE, 1)
    rotated = rotate(jnp.concatenate(sort_rows(rope_rows), 0))
    packed = jnp.where(lane[:GROUP] < ROPE, rotated[:GROUP], rotated[GROUP:]).astype(jnp.bfloat16)
    for at in range(4):
        kbuf[at // 2, 0, GROUP : GROUP + 16, (at % 2) * 128 : (at % 2 + 1) * 128] = packed[
            at * 16 : (at + 1) * 16
        ]

    pl.semaphore_wait(barrier, len(peers))

    def ring_block(offset, kind, other=False):
        if kind == "full":
            return kbuf.at[c, SLOT[offset]]
        parity = lax.rem(x, 2)
        first = (1 - parity if other else parity) * (HALF // 2)
        return kbuf.at[c, SLOT[offset], :, pl.ds(pl.multiple_of(first, 128), HALF // 2)]

    def ring_copy(kind, offset, arriving=False):
        side = kind == "side"
        sem = (SHARDS if side else 0) + SLOT[offset]
        return pltpu.make_async_remote_copy(
            src_ref=ring_block(offset if side else TREE[offset], kind, arriving and side),
            dst_ref=ring_block(offset, kind, arriving and side),
            send_sem=ring_send.at[sem],
            recv_sem=ring_recv.at[sem],
            device_id=x_peer(SIDES[offset]) if side else ring_peer(step_of(offset, TREE[offset])),
            device_id_type=MESH,
        )

    ring = {send: ring_copy(*send) for send in SENDS}

    def hand_on(kind, offset):
        for send in SENDS:
            if send[0] == "side":
                if kind == "half" and send[1] == offset:
                    ring[send].start()
            elif kind != "side" and TREE[send[1]] == offset:
                ring[send].start()

    hand_on("full", (0, 0))

    def pair_copy(first, count):
        rows = kbuf.at[c, pl.ds(first, count)]
        return pltpu.make_async_remote_copy(
            src_ref=rows,
            dst_ref=rows,
            send_sem=pair_send.at[first],
            recv_sem=pair_recv.at[first],
            device_id=partner,
            device_id_type=MESH,
        )

    spans = [(max(1, at), min(at + BATCH, SHARDS) - max(1, at)) for at in range(0, LAST, BATCH)]
    spans += [(at, 1) for at in range(LAST, SHARDS)]
    pairs = {first + count - 1: pair_copy(first, count) for first, count in spans}

    key_lane = lax.broadcasted_iota(jnp.int32, (1, BATCH * GROUP), 1)

    def mask_row(offsets, visible):
        line = jnp.zeros((1, BATCH * GROUP), jnp.float32)
        for at, (dy, dz) in enumerate(offsets):
            if (dy, dz) != (0, 0):
                owner = lax.rem(z - dz + NZ, NZ) * NY + lax.rem(y - dy + NY, NY)
                key_low = jnp.minimum(order[2 * owner], order[2 * owner + 1])
                here = key_lane // GROUP == at
                line = jnp.where(here, jnp.where(visible(key_low), 0.0, HIDDEN), line)
        return line

    for batch in range(BATCHES):
        span = slice(batch * BATCH, (batch + 1) * BATCH)
        bias[batch, 0:1, :] = mask_row(OFFSETS[span], lambda key_low: key_low < low)
        bias[batch, 8:9, :] = mask_row(OFFSETS[span], lambda key_low: key_low > low)

    top[...] = jnp.full_like(top, HIDDEN)
    total[...] = jnp.zeros_like(total)

    @pl.loop(0, ROWS // GROUP)
    def _(at):
        acc[pl.ds(at * GROUP, GROUP), :] = jnp.zeros((GROUP, LATENT), jnp.float32)

    loads[2].wait()
    for block in range(HEADS // 2):
        rows = qr[:, block * 128 : (block + 1) * 128].astype(jnp.float32)
        rotated = rotate(jnp.concatenate(sort_rows(rows), 0)) * SCORE_SCALE
        shifted = pltpu.roll(rotated, ROPE, 1)
        for odd in range(2):
            head = 2 * block + odd
            for_low = jnp.where(lane < ROPE, shifted if odd else rotated, 0.0).astype(jnp.bfloat16)
            for_high = jnp.where(lane < ROPE, 0.0, rotated if odd else shifted).astype(jnp.bfloat16)
            at = head * GROUP
            qa[at : at + GROUP, LATENT:] = for_low[:GROUP]
            qa[ROWS // 2 + at : ROWS // 2 + at + GROUP, LATENT:] = for_low[GROUP:]
            qb[at : at + GROUP, LATENT:] = for_high[GROUP:]
    loads[1].wait()
    loads[3].wait()
    for head in range(HEADS):
        rows = jnp.concatenate(sort_rows(qn[:, head * NOPE : (head + 1) * NOPE]), 0)
        absorbed = jnp.dot(rows, wuk[head], preferred_element_type=jnp.float32) * SCORE_SCALE
        absorbed = absorbed.astype(jnp.bfloat16)
        at = head * GROUP
        qa[at : at + GROUP, :LATENT] = absorbed[:GROUP]
        qa[ROWS // 2 + at : ROWS // 2 + at + GROUP, :LATENT] = absorbed[GROUP:]
        qb[at : at + GROUP, :LATENT] = absorbed[GROUP:]

    def soften(rows, scores):
        pieces = [s[:, at : at + 128] for s in scores for at in range(0, s.shape[1], 128)]
        peak = functools.reduce(jnp.maximum, pieces)
        before = top[rows, :]
        now = jnp.maximum(before, jnp.max(peak, 1, keepdims=True))
        fade = jnp.exp2(before - now)
        weights = [jnp.exp2(piece - now) for piece in pieces]
        top[rows, :] = now
        total[rows, :] = total[rows, :] * fade + functools.reduce(jnp.add, weights)
        return fade, [w.astype(jnp.bfloat16) for w in weights]

    def gain(rows, softened, values):
        fade, weights = softened
        summed = None
        per = len(weights) // len(values)
        for at, value in enumerate(values):
            mine = jnp.concatenate(weights[at * per : (at + 1) * per], 1)
            part_sum = jnp.dot(mine, value[:, :LATENT], preferred_element_type=jnp.float32)
            summed = part_sum if summed is None else summed + part_sum
        for at in range(0, LATENT, 128):
            acc[rows, at : at + 128] = acc[rows, at : at + 128] * fade + summed[:, at : at + 128]

    def gather_keys(batch):
        for at in range(BATCH):
            slot = batch * BATCH + at
            rows = slice(at * GROUP, (at + 1) * GROUP)
            for half in range(2):
                cols = slice(half * HALF, (half + 1) * HALF)
                klo[rows, cols] = kbuf[half, slot, 0:GROUP, :]
                khi[rows, cols] = kbuf[half, slot, GROUP + 16 : MSG, :]
            for piece in range(4):
                rotary = kbuf[
                    piece // 2, slot, GROUP : GROUP + 16, (piece % 2) * 128 : (piece % 2 + 1) * 128
                ]
                at_row = at * GROUP + piece * 16
                klo[at_row : at_row + 16, LATENT:] = rotary
                khi[at_row : at_row + 16, LATENT:] = rotary

    def own_mask(scores):
        key = lax.broadcasted_iota(jnp.int32, scores.shape, 1)
        token = lax.rem(lax.broadcasted_iota(jnp.int32, scores.shape, 0), GROUP)
        return jnp.where((key < GROUP) & (key > token), HIDDEN, scores)

    low_rows, high_rows = pl.ds(0, ROWS // 2), pl.ds(ROWS // 2, ROWS // 2)

    def attend(batch, between=()):
        for slot in range(batch * BATCH, (batch + 1) * BATCH):
            if slot in pairs:
                pairs[slot].wait_recv()
        gather_keys(batch)

        def low_low(rows=low_rows):
            scores = dot_nt(qa[rows, :], klo[...]) + bias[batch, 0:1, :]
            return own_mask(scores) if batch == 0 else scores

        def high_low(rows=high_rows):
            return dot_nt(qa[rows, :], klo[...])

        def high_high(rows=pl.ds(0, ROWS // 2)):
            scores = dot_nt(qb[rows, :], khi[...]) + bias[batch, 8:9, :]
            return own_mask(scores) if batch == 0 else scores

        n = ROWS // 4
        a, b = pl.ds(0, n), pl.ds(n, n)
        ha, hb = pl.ds(2 * n, n), pl.ds(3 * n, n)
        la = low_low(a)
        lb = low_low(b)
        wa = soften(a, [la])
        hla, hha = high_low(ha), high_high(a)
        wb = soften(b, [lb])
        gain(a, wa, [klo])
        hlb, hhb = high_low(hb), high_high(b)
        wha = soften(ha, [hla, hha])
        gain(b, wb, [klo])
        for step in between:
            run(step)
        whb = soften(hb, [hlb, hhb])
        gain(ha, wha, [klo, khi])
        gain(hb, whb, [klo, khi])

    def column(core, piece):
        return pl.multiple_of(core * COLS + piece * PIECE, 128)

    def exchange_copy(group, piece):
        return pltpu.make_async_remote_copy(
            src_ref=xsend.at[group, piece],
            dst_ref=xrecv.at[group, piece],
            send_sem=ex_send.at[group, piece],
            recv_sem=ex_recv.at[group, piece],
            device_id=partner,
            device_id_type=MESH,
        )

    def scatter_copy(group, piece, d):
        to = lax.rem(x + d, NX)
        return pltpu.make_async_remote_copy(
            src_ref=part.at[group, piece, pl.ds(pl.multiple_of(to * 16, 16), 16)],
            dst_ref=rsr.at[group, piece, d - 1],
            send_sem=rs_send.at[group, piece, d - 1],
            recv_sem=rs_recv.at[group, piece, d - 1],
            device_id=x_peer(d),
            device_id_type=MESH,
        )

    def out_piece(group, piece, chip):
        rows = pl.ds(pl.multiple_of(group * GROUP + chip * 16, 16), 16)
        return out.at[rows, pl.ds(column(c, piece), PIECE)]

    def share_copy(group, piece, d):
        block = out_piece(group, piece, x)
        return pltpu.make_async_remote_copy(
            src_ref=block,
            dst_ref=block,
            send_sem=ag_send.at[group, piece, d],
            recv_sem=ag_recv.at[group, piece, d],
            device_id=x_peer(d) if d else partner,
            device_id_type=MESH,
        )

    def forward_copy(group, piece, d):
        block = out_piece(group, piece, lax.rem(x + NX - d, NX))
        return pltpu.make_async_remote_copy(
            src_ref=block,
            dst_ref=block,
            send_sem=fw_send.at[group, piece, d - 1],
            recv_sem=fw_recv.at[group, piece, d - 1],
            device_id=partner,
            device_id_type=MESH,
        )

    def heads(group):
        if group == 0:
            loads[4].wait()
            loads[5].wait()
        for head in range(HEADS):
            rows = pl.ds(group * (ROWS // 2) + head * GROUP, GROUP)
            norm = 1.0 / jnp.sum(total[rows, :], 1, keepdims=True)
            context = (acc[rows, :] * norm).astype(jnp.bfloat16)
            flat[group * GROUP : (group + 1) * GROUP, head * VDIM : (head + 1) * VDIM] = jnp.dot(
                context, wuv[head], preferred_element_type=jnp.float32
            ).astype(jnp.bfloat16)

    def to_slots():
        first, second = sort_rows(flat[...])
        flat[:GROUP], flat[GROUP:] = first, second

    def partial_out(core, piece):
        return jnp.dot(
            flat[...], op[:, pl.ds(column(core, piece), PIECE)], preferred_element_type=jnp.float32
        )

    def exchange(piece):
        sums = partial_out(1 - c, piece).astype(jnp.bfloat16)
        for group in range(2):
            xsend[group, piece] = sums[group * GROUP : (group + 1) * GROUP]
            exchange_copy(group, piece).start()

    def keep(piece):
        sums = partial_out(c, piece)
        for group in range(2):
            own[group, piece] = sums[group * GROUP : (group + 1) * GROUP]

    def scatter(group, piece):
        exchange_copy(group, piece).wait_recv()
        summed = own[group, piece] + xrecv[group, piece].astype(jnp.float32)
        own[group, piece] = summed
        part[group, piece] = summed.astype(jnp.bfloat16)
        for d in (2, 1, 3):
            scatter_copy(group, piece, d).start()

    def share(group, piece):
        for d in (1, 2, 3):
            scatter_copy(group, piece, d).wait_recv()
        summed = own[group, piece, pl.ds(pl.multiple_of(x * 16, 16), 16), :]
        for d in range(3):
            summed = summed + rsr[group, piece, d].astype(jnp.float32)
        rows = pl.ds(pl.multiple_of(group * GROUP + x * 16, 16), 16)
        out[rows, pl.ds(column(c, piece), PIECE)] = summed.astype(jnp.bfloat16)
        for d in (2, 1, 3, 0):
            share_copy(group, piece, d).start()

    def forward(group, piece):
        for d in (1, 3, 2):
            share_copy(group, piece, d).wait_recv()
            forward_copy(group, piece, d).start()

    def settle_output():
        for group in range(2):
            for piece in range(PIECES):
                exchange_copy(group, piece).wait_send()
                for d in (1, 2, 3):
                    scatter_copy(group, piece, d).wait_send()

    def settle_gather():
        for send in SENDS:
            ring[send].wait_send()
        for pair in pairs.values():
            pair.wait_send()

    def arrive(kind, offset):
        (ring_copy(kind, offset, True) if kind == "side" else ring[kind, offset]).wait_recv()
        hand_on(kind, offset)
        if kind != "half" and SLOT[offset] in pairs:
            pairs[SLOT[offset]].start()

    steps = {
        "attend": attend,
        "heads": heads,
        "exchange": exchange,
        "keep": keep,
        "scatter": scatter,
        "share": share,
        "forward": forward,
        "slots": to_slots,
        "settle_gather": settle_gather,
        "settle_output": settle_output,
    }

    def run(step):
        if step[0] in steps:
            steps[step[0]](*step[1:])
        else:
            arrive(*step)

    for step in PLAN:
        run(step)

    tail = [(group, piece) for group in range(2) for piece in range(PIECES)]
    for group, piece in tail:
        share_copy(group, piece, 0).wait_recv()
        for d in (1, 2, 3):
            forward_copy(group, piece, d).wait_recv()
    for group, piece in tail:
        for d in (0, 1, 2, 3):
            share_copy(group, piece, d).wait_send()
        for d in (1, 2, 3):
            forward_copy(group, piece, d).wait_send()


def on_device(q_nope, q_rope, latent_keys, group_order, w_uk, w_uv, o_proj):
    bf16, f32 = jnp.bfloat16, jnp.float32
    anywhere = pl.BlockSpec(memory_space=pl.ANY)
    vmem, dma = pltpu.VMEM, pltpu.SemaphoreType.DMA
    rows = pl.pallas_call(
        attention_kernel,
        out_shape=pltpu.VMEM((TOK, OUT), bf16),
        in_specs=[pl.BlockSpec(memory_space=pltpu.SMEM)] + [anywhere] * 6,
        out_specs=pl.BlockSpec(memory_space=pltpu.VMEM),
        scratch_shapes=[
            vmem((TOK, HEADS * NOPE), bf16),
            vmem((TOK, HEADS * ROPE), bf16),
            vmem((LATENT + ROPE, TOK), bf16),
            vmem((HEADS, NOPE, LATENT), bf16),
            vmem((HEADS, LATENT, VDIM), bf16),
            vmem((HEADS * VDIM, OUT), bf16),
            vmem((TOK, 128), f32),
            vmem((2, SHARDS, MSG, HALF), bf16),
            vmem((ROWS, KW), bf16),
            vmem((ROWS // 2, KW), bf16),
            vmem((BATCH * GROUP, KW), bf16),
            vmem((BATCH * GROUP, KW), bf16),
            vmem((BATCHES, 16, BATCH * GROUP), f32),
            vmem((ROWS, 128), f32),
            vmem((ROWS, 128), f32),
            vmem((ROWS, LATENT), f32),
            vmem((TOK, HEADS * VDIM), bf16),
            vmem((2, PIECES, GROUP, PIECE), bf16),
            vmem((2, PIECES, GROUP, PIECE), bf16),
            vmem((2, PIECES, GROUP, PIECE), f32),
            vmem((2, PIECES, GROUP, PIECE), bf16),
            vmem((2, PIECES, 3, 16, PIECE), bf16),
            dma((6,)),
            dma((2 * SHARDS,)),
            dma((2 * SHARDS,)),
            dma((SHARDS,)),
            dma((SHARDS,)),
            dma((2, PIECES)),
            dma((2, PIECES)),
            dma((2, PIECES, 3)),
            dma((2, PIECES, 3)),
            dma((2, PIECES, 4)),
            dma((2, PIECES, 4)),
            dma((2, PIECES, 3)),
            dma((2, PIECES, 3)),
        ],
        compiler_params=pltpu.CompilerParams(
            collective_id=0, has_side_effects=True, vmem_limit_bytes=56 * 1024 * 1024
        ),
    )(
        group_order,
        q_nope.reshape(TOK, HEADS * NOPE),
        q_rope.reshape(TOK, HEADS * ROPE),
        jnp.transpose(latent_keys, (0, 2, 1)).reshape(LATENT + ROPE, TOK),
        w_uk,
        w_uv,
        o_proj,
    )
    return rows.reshape(1, TOK, OUT)


def solution(mesh):
    placed = (
        P(None, "ctx", "tp"),
        P(None, "ctx", "tp"),
        P(None, "ctx", None),
        P(),
        P("tp", None, None),
        P("tp", None, None),
        P("tp", None),
    )
    return jax.shard_map(
        on_device, mesh=mesh, in_specs=placed, out_specs=P(None, "ctx", None), check_vma=False
    )
```
